128 devices in a mesh: gx: 8 (over z_lo, x), gy: 16 (over y, z_hi, core).
Axes of the slice: x: 4, y: 4, z: 4 (z_hi: 2, z_lo: 2; z = z_hi * 2 + z_lo), core: 2. Of those that a mesh axis runs over, the one named last changes fastest.
Arguments:
- point_feats: bfloat16 [524288, 128], P(('gx', 'gy')), may hold values from -6 to 6
- top_bin: int32 [524288], P(('gx', 'gy')), may hold values from -1 to 131071, as said below
- front_bin: int32 [524288], P(('gx', 'gy')), may hold values from -1 to 16383, as said below
- side_bin: int32 [524288], P(('gx', 'gy')), may hold values from -1 to 8191, as said below
- camera_of_device: int32 [128], P(('gx', 'gy')), may hold values from 0 to 5
- camera_embed: float32 [6, 128], replicated, may hold values from -6 to 6
- w_in: bfloat16 [128, 256], replicated, may hold values from -0.5 to 0.5
- b_in: float32 [256], replicated, may hold values from -6 to 6
- w_out: bfloat16 [256, 128], replicated, may hold values from -0.375 to 0.375
- b_out: float32 [128], replicated, may hold values from -3 to 3
Outputs:
- voxels: bfloat16 [512, 256, 32, 128], P('gx', 'gy')
The draws below stay inside these ranges and needn't reach their ends.
Inputs may be any that keep to these rules, and one draw needn't show every extreme that they name: For each point, top_bin, front_bin and side_bin are all -1, or all describe the same cell (x, y, z): top_bin = x * 256 + y, front_bin = x * 32 + z, side_bin = y * 32 + z. Of the points of one device, at most 64 lie in the block of x cells [i * 64, (i + 1) * 64) and y cells [j * 16, (j + 1) * 16) of any one pair (i, j); in every draw some such block receives exactly 64 points from every device. `front_bin`: see top_bin. `side_bin`: see top_bin.
All inputs are finite; a program needn't handle non-finite values.
Results may differ from the reference program's by a relative error of at most 0.001.
The reference program's roundings to bfloat16 on the way (of `features`, `top`, `front`, `side`, `cell` and `hidden`) count: a program that leaves them out, or rounds other values in their place, can miss the bound.
Values may be sent and summed in bfloat16 or wider, within the bound.
No kernel may reach another device: no remote copies, remote signals or barrier semaphores. Data moves between devices by JAX's collectives and lax.ppermute only.
A program may use at most 64 MiB of HBM per device.

```python
import jax
import jax.numpy as jnp
from jax import lax

C = 128
HID = 256
CAMS = 6
NZ = 32
BX = 64
BY = 16
P_DEV = 4096
NX = 512
NY = 256
TOTAL_POINTS = 524288
CAP = 64
N_GY = 16
DEVICES = 128


def route_points(key):
    owner_key, fixed_key, cell_key, order_key = jax.random.split(key, 4)
    loads = jax.random.randint(owner_key, (DEVICES, DEVICES), CAP // 4, 3 * CAP // 4)
    forced = jax.random.randint(fixed_key, (), 0, DEVICES)
    owners = jnp.arange(DEVICES)
    loads = jnp.where(owners[None, :] == forced, CAP, loads)
    rolled = jnp.roll(loads, -forced, axis=1)
    bounds = jnp.cumsum(rolled, axis=1)
    position = jnp.arange(P_DEV)
    slot_owner = jax.vmap(lambda edges: jnp.searchsorted(edges, position, side='right'))(bounds)
    order = jax.vmap(lambda sub: jax.random.permutation(sub, P_DEV))(jax.random.split(order_key, DEVICES))
    slot_owner = jnp.take_along_axis(slot_owner, order, axis=1)
    live = slot_owner < DEVICES
    owner = (slot_owner + forced) % DEVICES
    key_x, key_y, key_z = jax.random.split(cell_key, 3)
    local_x = jax.random.randint(key_x, (DEVICES, P_DEV), 0, BX)
    local_y = jax.random.randint(key_y, (DEVICES, P_DEV), 0, BY)
    depth = jax.random.randint(key_z, (DEVICES, P_DEV), 0, NZ)
    grid_x = owner // N_GY * BX + local_x
    grid_y = owner % N_GY * BY + local_y
    top = jnp.where(live, grid_x * NY + grid_y, -1).reshape(-1).astype(jnp.int32)
    front = jnp.where(live, grid_x * NZ + depth, -1).reshape(-1).astype(jnp.int32)
    side = jnp.where(live, grid_y * NZ + depth, -1).reshape(-1).astype(jnp.int32)
    return (top, front, side)


def draw_top_bin(key, part):
    shared = route_points(key)
    return shared[0]


def draw_front_bin(key, part):
    shared = route_points(key)
    return shared[1]


def draw_side_bin(key, part):
    shared = route_points(key)
    return shared[2]


def place_ends(array, key, low, largest):
    longest = array.shape.index(max(array.shape))
    spots = []
    for shift in (0, 1):
        where = [jax.random.randint(jax.random.fold_in(key, axis), (), 0, length) for axis, length in enumerate(array.shape)]
        where[longest] = (where[longest] + shift) % array.shape[longest]
        spots.append(tuple(where))
    return array.at[spots[0]].set(low).at[spots[1]].set(largest)


def shard_levels(rng, shape, cuts, least, largest):
    factor_of = 1.0
    for dim, blocks in cuts:
        heights = jax.random.uniform(jax.random.fold_in(jax.random.fold_in(rng, 6), dim), (blocks,), jnp.float32, least / len(cuts), largest / len(cuts))
        factor_of = factor_of * jnp.repeat(jnp.exp(heights), shape[dim] // blocks).reshape((-1,) + (1,) * (len(shape) - 1 - dim))
    return factor_of


def noise(own_key, dims, deviation, most, cuts=(), kind=jnp.bfloat16):
    drawn = deviation * jax.random.normal(own_key, dims, jnp.float32)
    if cuts:
        drawn = drawn * shard_levels(own_key, dims, cuts, -0.22, 0.18)
    return jnp.clip(drawn, -most, most).astype(kind)


def setup_inputs(seed: int = 0) -> dict:
    keys = jax.random.split(jax.random.key(seed), 11)
    point_feats = noise(keys[0], (TOTAL_POINTS, C), 1.0, 6.0, ((0, 128),))
    top_bin = draw_top_bin(jax.random.fold_in(keys[10], 71), 0)
    front_bin = draw_front_bin(jax.random.fold_in(keys[10], 71), 0)
    side_bin = draw_side_bin(jax.random.fold_in(keys[10], 71), 0)
    camera_of_device = place_ends(jax.random.randint(keys[4], (DEVICES,), 0, CAMS), jax.random.fold_in(keys[4], 1), 0, CAMS - 1).astype(jnp.int32)
    camera_embed = noise(keys[5], (CAMS, C), 1.0, 6.0, (), jnp.float32)
    w_in = noise(keys[6], (C, HID), C ** -0.5, 0.5)
    b_in = noise(keys[7], (HID,), 1.0, 6.0, (), jnp.float32)
    w_out = noise(keys[8], (HID, C), HID ** -0.5, 0.375)
    b_out = noise(keys[9], (C,), 0.5, 3.0, (), jnp.float32)
    return {"point_feats": point_feats, "top_bin": top_bin, "front_bin": front_bin, "side_bin": side_bin, "camera_of_device": camera_of_device, "camera_embed": camera_embed, "w_in": w_in, "b_in": b_in, "w_out": w_out, "b_out": b_out}


def pool_plane(features, bins, cells):
    safe = jnp.where(bins >= 0, bins, cells).astype(jnp.int32)
    summed = jax.ops.segment_sum(features.astype(jnp.float32), safe, num_segments=cells + 1)
    return summed[:cells].astype(jnp.bfloat16)


def reference(point_feats, top_bin, front_bin, side_bin, camera_of_device, camera_embed, w_in, b_in, w_out, b_out):
    device_of_point = (jnp.arange(TOTAL_POINTS) // P_DEV).astype(jnp.int32)
    camera = camera_of_device[device_of_point]
    features = (point_feats.astype(jnp.float32) + camera_embed[camera]).astype(jnp.bfloat16)
    top = pool_plane(features, top_bin, NX * NY).reshape(NX, NY, C)
    front = pool_plane(features, front_bin, NX * NZ).reshape(NX, NZ, C)
    side = pool_plane(features, side_bin, NY * NZ).reshape(NY, NZ, C)

    def mix(parts):
        top_rows, front_rows = parts
        cell = (top_rows[:, :, None, :].astype(jnp.float32) + front_rows[:, None, :, :].astype(jnp.float32)
                + side[None, :, :, :].astype(jnp.float32)).astype(jnp.bfloat16)
        flat = cell.reshape(-1, C)
        hidden = jax.nn.gelu(jnp.dot(flat, w_in, preferred_element_type=jnp.float32) + b_in, approximate=False).astype(jnp.bfloat16)
        result = jnp.dot(hidden, w_out, preferred_element_type=jnp.float32) + b_out + flat.astype(jnp.float32)
        return result.astype(jnp.bfloat16).reshape(4, NY, NZ, C)

    blocks = lax.map(mix, (top.reshape(NX // 4, 4, NY, C), front.reshape(NX // 4, 4, NZ, C)))
    return blocks.reshape(NX, NY, NZ, C)
```

```python
import jax
import jax.numpy as jnp
from jax import lax
from jax.experimental import pallas as pl
from jax.experimental.pallas import tpu as pltpu
from jax.sharding import PartitionSpec as P

C = 128
HID = 256
CAMS = 6
NZ = 32
BX = 64
BY = 16
P_DEV = 4096
DEVICES = 128
N_GX = 8
N_GY = 16
CAP = 64
ROWS = CAP + 8
SLOTS = DEVICES * CAP
CHUNKS = P_DEV // 128
PAIRS = DEVICES // 2

F32 = jnp.float32
BF16 = jnp.bfloat16
VMEM_LIMIT = 48 * 2**20


def iota(shape, axis):
    return lax.broadcasted_iota(jnp.int32, shape, axis)


def columns_of(row):
    diagonal = jnp.where(iota((128, 128), 0) == iota((128, 128), 1), row, 0.0).astype(BF16)
    return jnp.dot(diagonal, jnp.ones((128, 128), BF16), preferred_element_type=F32)


def split_columns(values, half):
    zero = jnp.zeros_like(values)
    return jnp.concatenate(
        [jnp.where(half < 0.5, values, zero), jnp.where(half < 0.5, zero, values)], axis=1
    )


def onehot_block(labels_ref, block, chunks):
    base = (block * 256).astype(F32) if not isinstance(block, int) else float(block * 256)
    numbers = iota((256, 128), 0).astype(F32).astype(BF16)
    one = jnp.ones((256, 128), BF16)
    zero = jnp.zeros((256, 128), BF16)
    pieces = []
    for k in range(chunks):
        label = labels_ref[pl.ds(k, 1), :] - base
        label = jnp.where((label >= 0.0) & (label < 256.0), label, -1.0)
        label = jnp.broadcast_to(label, (256, 128)).astype(BF16)
        pieces.append(jnp.where(label == numbers, one, zero))
    return jnp.concatenate(pieces, axis=1)


def pack_kernel(cam_ref, feats_ref, top_ref, front_ref, embed_ref, out_ref, rank_ref, label_ref, half_ref, rhs_ref, meta_ref):
    top = top_ref[...]
    live = top >= 0
    grid_x = top >> 8
    grid_y = top & 255
    owner = jnp.where(live, (grid_x >> 6) * N_GY + (grid_y >> 4), -1)
    local_x = (grid_x & (BX - 1)).astype(F32) + 1.0
    local_y = (grid_y & (BY - 1)).astype(F32) + 1.0
    depth = (front_ref[...] & (NZ - 1)).astype(F32) + 1.0

    before = iota((128, 256), 0) < iota((128, 256), 1)
    later = iota((128, 256), 1) >= 128
    counter = jnp.where(before | later, 1.0, 0.0).astype(BF16)
    seen = jnp.zeros((DEVICES, 128), F32)
    meta = jnp.zeros((DEVICES, 3 * 128), F32)
    slot_of_row = (iota((128, 128), 0) & (CAP - 1)).astype(F32)
    for k in range(CHUNKS):
        mine = iota((DEVICES, 128), 0) == owner[k : k + 1, :]
        marks = jnp.where(mine, 1.0, 0.0).astype(BF16)
        counts = jnp.dot(marks, counter, preferred_element_type=F32)
        rank = jnp.sum(jnp.where(mine, counts[:, :128] + seen, 0.0), axis=0, keepdims=True)
        seen = seen + counts[:, 128:]
        rank_ref[pl.ds(k, 1), :] = rank
        here = slot_of_row == rank
        values = jnp.concatenate(
            [
                jnp.where(here, local_x[k : k + 1, :], 0.0),
                jnp.where(here, local_y[k : k + 1, :], 0.0),
                jnp.where(here, depth[k : k + 1, :], 0.0),
            ],
            axis=0,
        ).astype(BF16)
        meta = meta + lax.dot_general(
            marks, values, (((1,), (1,)), ((), ())), preferred_element_type=F32
        )
    rank = rank_ref[...].astype(jnp.int32)
    label_ref[...] = jnp.where(live, owner * (CAP // 2) + (rank & (CAP // 2 - 1)), -1).astype(F32)
    half_ref[...] = (rank >> 5).astype(F32)

    for part in range(3):
        meta_ref[pl.ds(part, DEVICES, stride=8), :] = meta[:, part * 128 : (part + 1) * 128]
    for part in range(3, 8):
        meta_ref[pl.ds(part, DEVICES, stride=8), :] = jnp.zeros((DEVICES, 128), F32)
    out_ref[:, CAP:ROWS, :] = meta_ref[...].reshape(DEVICES, 8, 128).astype(BF16)

    camera = embed_ref[pl.ds(cam_ref[0], 1), :]

    @pl.loop(0, CHUNKS)
    def _(k):
        rows = pl.ds(pl.multiple_of(k * 128, 128), 128)
        features = (feats_ref[rows, :].astype(F32) + camera).astype(BF16)
        half = columns_of(half_ref[pl.ds(k, 1), :])
        rhs_ref[rows, :] = split_columns(features.astype(F32), half).astype(BF16)

    @pl.loop(0, SLOTS // 512)
    def _(block):
        picked = jnp.dot(
            onehot_block(label_ref, block, CHUNKS), rhs_ref[...], preferred_element_type=F32
        ).astype(BF16)
        devices = pl.ds(block * 8, 8)
        out_ref[devices, 0 : CAP // 2, :] = picked[:, :C].reshape(8, CAP // 2, C)
        out_ref[devices, CAP // 2 : CAP, :] = picked[:, C:].reshape(8, CAP // 2, C)


def pack(camera, point_feats, top_bin, front_bin, camera_embed):
    whole = pl.BlockSpec(memory_space=pltpu.VMEM)
    return pl.pallas_call(
        pack_kernel,
        out_shape=jax.ShapeDtypeStruct((DEVICES, ROWS, C), BF16),
        in_specs=[pl.BlockSpec(memory_space=pltpu.SMEM)] + [whole] * 4,
        out_specs=whole,
        scratch_shapes=[
            pltpu.VMEM((CHUNKS, 128), F32),
            pltpu.VMEM((CHUNKS, 128), F32),
            pltpu.VMEM((CHUNKS, 128), F32),
            pltpu.VMEM((P_DEV, 2 * C), BF16),
            pltpu.VMEM((DEVICES * 8, 128), F32),
        ],
        compiler_params=pltpu.CompilerParams(vmem_limit_bytes=VMEM_LIMIT),
        cost_estimate=pl.CostEstimate(flops=2 * 4096 * 4096 * 256, bytes_accessed=4 * 2**20, transcendentals=0),
        name="pack",
    )(camera, point_feats, top_bin.reshape(CHUNKS, 128), front_bin.reshape(CHUNKS, 128), camera_embed)


def pool_kernel(got_ref, front_ref, side_ref, top_ref, meta_ref, fl_ref, sl_ref, tl_ref, zh_ref, yh_ref, zr_ref, yr_ref):
    meta_ref[...] = got_ref[:, CAP:ROWS, :].astype(F32).reshape(DEVICES * 8, 128)
    first = iota((PAIRS, 128), 1) < CAP

    def pairs(part):
        even = meta_ref[pl.ds(part, PAIRS, stride=16), :]
        odd = meta_ref[pl.ds(part + 8, PAIRS, stride=16), :]
        return jnp.where(first, even, odd).astype(jnp.int32) - 1

    x, y, z = pairs(0), pairs(1), pairs(2)
    live = x >= 0
    fl_ref[...] = jnp.where(live, x * 16 + (z & 15), -1).astype(F32)
    sl_ref[...] = jnp.where(live, y * 16 + (z & 15), -1).astype(F32)
    tl_ref[...] = jnp.where(live, x * 8 + (y & 7), -1).astype(F32)
    zh_ref[...] = ((z >> 4) & 1).astype(F32)
    yh_ref[...] = ((y >> 3) & 1).astype(F32)

    @pl.loop(0, PAIRS)
    def _(q):
        rows = pl.ds(pl.multiple_of(q * 128, 128), 128)
        piece = got_ref[pl.ds(q * 2, 2), 0:CAP, :].reshape(128, C).astype(F32)
        zr_ref[rows, :] = split_columns(piece, columns_of(zh_ref[pl.ds(q, 1), :])).astype(BF16)
        yr_ref[rows, :] = split_columns(piece, columns_of(yh_ref[pl.ds(q, 1), :])).astype(BF16)

    @pl.loop(0, 4)
    def _(block):
        sums = jnp.dot(onehot_block(fl_ref, block, PAIRS), zr_ref[...], preferred_element_type=F32)
        xs = pl.ds(block * 16, 16)
        front_ref[xs, 0:16, :] = sums[:, :C].reshape(16, 16, C)
        front_ref[xs, 16:32, :] = sums[:, C:].reshape(16, 16, C)

    sums = jnp.dot(onehot_block(sl_ref, 0, PAIRS), zr_ref[...], preferred_element_type=F32)
    side_ref[:, 0:16, :] = sums[:, :C].reshape(16, 16, C)
    side_ref[:, 16:32, :] = sums[:, C:].reshape(16, 16, C)

    @pl.loop(0, 2)
    def _(block):
        sums = jnp.dot(onehot_block(tl_ref, block, PAIRS), yr_ref[...], preferred_element_type=F32)
        xs = pl.ds(block * 32, 32)
        top_ref[xs, 0:8, :] = sums[:, :C].reshape(32, 8, C)
        top_ref[xs, 8:16, :] = sums[:, C:].reshape(32, 8, C)


def pool(got):
    whole = pl.BlockSpec(memory_space=pltpu.VMEM)
    return pl.pallas_call(
        pool_kernel,
        out_shape=[
            jax.ShapeDtypeStruct((BX, NZ, C), F32),
            jax.ShapeDtypeStruct((BY, NZ, C), F32),
            jax.ShapeDtypeStruct((BX, BY, C), F32),
        ],
        in_specs=[whole],
        out_specs=[whole] * 3,
        scratch_shapes=[pltpu.VMEM((DEVICES * 8, 128), F32)]
        + [pltpu.VMEM((PAIRS, 128), F32)] * 5
        + [pltpu.VMEM((SLOTS, 2 * C), BF16)] * 2,
        compiler_params=pltpu.CompilerParams(vmem_limit_bytes=VMEM_LIMIT),
        cost_estimate=pl.CostEstimate(flops=2 * 8192 * 1792 * 256, bytes_accessed=4 * 2**20, transcendentals=0),
        name="pool",
    )(got)


ATANH_ERF = (
    0.7978842164012749,
    0.036334282759596444,
    -3.312947161090104e-05,
    -5.524030501873291e-05,
    3.9691284083295496e-06,
    -1.3344752372813232e-07,
    1.80564030499361e-09,
)


def gelu(x):
    square = jnp.minimum(x * x, 64.0)
    ratio = ATANH_ERF[-1] * square + ATANH_ERF[-2]
    for factor in ATANH_ERF[-3::-1]:
        ratio = ratio * square + factor
    half = 0.5 * x
    return half + half * jnp.tanh(x * ratio)


STEP = 4


def mlp_kernel(top_ref, front_ref, side_ref, w_in_ref, b_in_ref, w_out_ref, b_out_ref, out_ref):
    for i in range(STEP):
        top = top_ref[i].astype(BF16).astype(F32)
        front = front_ref[i].astype(F32)
        cell = (top[:, None, :] + front[None, :, :] + side_ref[...].astype(F32)).astype(BF16)
        cell = cell.reshape(BY * NZ, C)
        hidden = jnp.dot(cell, w_in_ref[...], preferred_element_type=F32) + b_in_ref[...]
        hidden = gelu(hidden).astype(BF16)
        result = jnp.dot(hidden, w_out_ref[...], preferred_element_type=F32)
        result = result + b_out_ref[...] + cell.astype(F32)
        out_ref[i] = result.astype(BF16).reshape(BY, NZ, C)


def mlp(top, front, side, w_in, b_in, w_out, b_out):
    def same(*shape):
        return pl.BlockSpec(shape, lambda i: (0,) * len(shape))

    return pl.pallas_call(
        mlp_kernel,
        grid=(BX // STEP,),
        in_specs=[
            pl.BlockSpec((STEP, BY, C), lambda i: (i, 0, 0)),
            pl.BlockSpec((STEP, NZ, C), lambda i: (i, 0, 0)),
            same(BY, NZ, C),
            same(C, HID),
            same(1, HID),
            same(HID, C),
            same(1, C),
        ],
        out_specs=pl.BlockSpec((STEP, BY, NZ, C), lambda i: (i, 0, 0, 0)),
        out_shape=jax.ShapeDtypeStruct((BX, BY, NZ, C), BF16),
        compiler_params=pltpu.CompilerParams(vmem_limit_bytes=VMEM_LIMIT),
        cost_estimate=pl.CostEstimate(
            flops=4 * BX * BY * NZ * C * HID, bytes_accessed=9 * 2**20, transcendentals=BX * BY * NZ * HID
        ),
        name="voxel_mlp",
    )(top, front, side, w_in, b_in.reshape(1, HID), w_out, b_out.reshape(1, C))


def plane_sum(part, axis, size):
    rows = part.shape[0] * part.shape[1] // size
    pieces = lax.all_to_all(part.reshape(size, rows, C), axis, 0, 0, tiled=True)
    share = jnp.sum(pieces, axis=0).astype(BF16)
    return lax.all_gather(share, axis, axis=0, tiled=True).reshape(part.shape)


def per_device(
    point_feats, top_bin, front_bin, side_bin, camera_of_device, camera_embed, w_in, b_in, w_out, b_out
):
    sent = pack(camera_of_device, point_feats, top_bin, front_bin, camera_embed)
    got = lax.all_to_all(sent, ("gx", "gy"), split_axis=0, concat_axis=0, tiled=True)
    front_part, side_part, top = pool(got)
    front = plane_sum(front_part, "gy", N_GY)
    side = plane_sum(side_part, "gx", N_GX)
    return mlp(top, front, side, w_in, b_in, w_out, b_out)


def solution(mesh):
    points = P(("gx", "gy"))
    placed = (P(("gx", "gy"), None), points, points, points, points, P(), P(), P(), P(), P())
    return jax.shard_map(
        per_device, mesh=mesh, in_specs=placed, out_specs=P("gx", "gy", None, None), check_vma=False
    )
```

```python
import jax
import jax.numpy as jnp
from jax import lax
from jax.experimental import pallas as pl
from jax.experimental.pallas import tpu as pltpu
from jax.sharding import PartitionSpec as P

C = 128
HID = 256
CAMS = 6
NZ = 32
BX = 64
BY = 16
P_DEV = 4096
DEVICES = 128
N_GX = 8
N_GY = 16
CAP = 64
ROWS = CAP + 8
SLOTS = DEVICES * CAP
CHUNKS = P_DEV // 128
PAIRS = DEVICES // 2

F32 = jnp.float32
BF16 = jnp.bfloat16
VMEM_LIMIT = 48 * 2**20


def iota(shape, axis):
    return lax.broadcasted_iota(jnp.int32, shape, axis)


def columns_of(row):
    diagonal = jnp.where(iota((128, 128), 0) == iota((128, 128), 1), row, 0.0).astype(BF16)
    return jnp.dot(diagonal, jnp.ones((128, 128), BF16), preferred_element_type=F32).astype(BF16)


def split_columns(values, half):
    zero = jnp.zeros_like(values)
    left = half == jnp.zeros_like(half)
    return jnp.concatenate([jnp.where(left, values, zero), jnp.where(left, zero, values)], axis=1)


def onehot_rows(label, base, rows):
    return jnp.where(iota((rows, 128), 0) + base == label, 1.0, 0.0).astype(BF16)


def onehot(labels_ref, base, rows, chunks):
    return jnp.concatenate(
        [onehot_rows(labels_ref[pl.ds(k, 1), :], base, rows) for k in range(chunks)], axis=1
    )


def pack_kernel(
    cam_ref, feats_ref, top_ref, front_ref, embed_ref, out_ref,
    marks_ref, rank_ref, place_ref, half_ref, rhs_ref, values_ref, sorted_ref, meta_ref, start_ref, start_smem, sem,
):
    top = top_ref[...]
    live = top >= 0
    grid_x = top >> 8
    grid_y = top & 255
    owner = jnp.where(live, (grid_x >> 6) * N_GY + (grid_y >> 4), -1)
    cells = (
        (grid_x & (BX - 1)) + 1,
        (grid_y & (BY - 1)) + 1,
        (front_ref[...] & (NZ - 1)) + 1,
    )
    cells = [cell.astype(F32) for cell in cells]

    for k in range(CHUNKS):
        marks_ref[:, k * 128 : (k + 1) * 128] = onehot_rows(owner[k : k + 1, :], 0, DEVICES)
    totals = jnp.dot(marks_ref[...], jnp.ones((P_DEV, 128), BF16), preferred_element_type=F32)
    below = jnp.where(iota((128, 128), 1) < iota((128, 128), 0), 1.0, 0.0).astype(BF16)
    starts = jnp.dot(below, totals.astype(BF16), preferred_element_type=F32)
    start_row = jnp.sum(
        jnp.where(iota((128, 128), 0) == iota((128, 128), 1), starts, 0.0), axis=0, keepdims=True
    )
    start_ref[...] = start_row.astype(jnp.int32)
    copy = pltpu.make_async_copy(start_ref, start_smem, sem)
    copy.start()

    before = iota((128, 256), 0) < iota((128, 256), 1)
    later = iota((128, 256), 1) >= 128
    counter = jnp.where(before | later, 1.0, 0.0).astype(BF16)
    seen = jnp.zeros((DEVICES, 128), F32)
    slot = iota((128, 128), 0) & (CAP - 1)
    for k in range(CHUNKS):
        columns = slice(k * 128, (k + 1) * 128)
        mine = iota((DEVICES, 128), 0) == owner[k : k + 1, :]
        counts = jnp.dot(marks_ref[:, columns], counter, preferred_element_type=F32)
        rank = jnp.sum(jnp.where(mine, counts[:, :128] + seen, 0.0), axis=0, keepdims=True)
        start = jnp.sum(jnp.where(mine, starts, 0.0), axis=0, keepdims=True)
        seen = seen + counts[:, 128:]
        place_ref[pl.ds(k, 1), :] = rank + start
        here = slot == rank.astype(jnp.int32)
        for part in range(3):
            values_ref[part * 128 : (part + 1) * 128, columns] = jnp.where(
                here, cells[part][k : k + 1, :], 0.0
            ).astype(BF16)
    place = place_ref[...].astype(jnp.int32)
    half_ref[...] = (place >> 11).astype(F32)
    place_ref[...] = jnp.where(live, place & 2047, -1).astype(F32)

    camera = embed_ref[pl.ds(cam_ref[0], 1), :]
    for k in range(CHUNKS):
        rows = slice(k * 128, (k + 1) * 128)
        features = (feats_ref[rows, :].astype(F32) + camera).astype(BF16)
        rhs_ref[rows, :] = split_columns(features, columns_of(half_ref[pl.ds(k, 1), :]))

    rank_ref[...] = place_ref[...].astype(jnp.int32)
    for block in range(8):
        base = block * 256
        picked = jnp.dot(onehot(rank_ref, base, 256, CHUNKS), rhs_ref[...], preferred_element_type=F32)
        sorted_ref[base : base + 256, :] = picked[:, :C]
        sorted_ref[2048 + base : 2304 + base, :] = picked[:, C:]
    sorted_ref[P_DEV : P_DEV + CAP, :] = jnp.zeros((CAP, C), F32)

    meta = lax.dot_general(
        values_ref[...], marks_ref[...], (((1,), (1,)), ((), ())), preferred_element_type=F32
    )
    for part in range(3):
        meta_ref[pl.ds(part, DEVICES, stride=8), :] = meta[part * 128 : (part + 1) * 128, :].T
    for part in range(3, 8):
        meta_ref[pl.ds(part, DEVICES, stride=8), :] = jnp.zeros((DEVICES, 128), F32)
    out_ref[:, CAP:ROWS, :] = meta_ref[...].reshape(DEVICES, 8, 128).astype(BF16)

    copy.wait()

    @pl.loop(0, DEVICES, unroll=8)
    def _(device):
        out_ref[device, 0:CAP, :] = sorted_ref[pl.ds(start_smem[0, device], CAP), :].astype(BF16)


def pack(camera, point_feats, top_bin, front_bin, camera_embed):
    whole = pl.BlockSpec(memory_space=pltpu.VMEM)
    return pl.pallas_call(
        pack_kernel,
        out_shape=jax.ShapeDtypeStruct((DEVICES, ROWS, C), BF16),
        in_specs=[pl.BlockSpec(memory_space=pltpu.SMEM)] + [whole] * 4,
        out_specs=whole,
        scratch_shapes=[
            pltpu.VMEM((DEVICES, P_DEV), BF16),
            pltpu.VMEM((CHUNKS, 128), jnp.int32),
            pltpu.VMEM((CHUNKS, 128), F32),
            pltpu.VMEM((CHUNKS, 128), F32),
            pltpu.VMEM((P_DEV, 2 * C), BF16),
            pltpu.VMEM((3 * 128, P_DEV), BF16),
            pltpu.VMEM((P_DEV + CAP, C), F32),
            pltpu.VMEM((DEVICES * 8, 128), F32),
            pltpu.VMEM((1, DEVICES), jnp.int32),
            pltpu.SMEM((1, DEVICES), jnp.int32),
            pltpu.SemaphoreType.DMA,
        ],
        compiler_params=pltpu.CompilerParams(vmem_limit_bytes=VMEM_LIMIT),
        cost_estimate=pl.CostEstimate(flops=2 * 4096 * 4096 * 256, bytes_accessed=4 * 2**20, transcendentals=0),
        name="pack",
    )(camera, point_feats, top_bin.reshape(CHUNKS, 128), front_bin.reshape(CHUNKS, 128), camera_embed)


def pool_side_kernel(half_ref, got_ref, side_ref, labels_ref, meta_ref):
    meta_ref[...] = got_ref[:, CAP:ROWS, :].astype(F32).reshape(DEVICES * 8, 128)
    first = iota((PAIRS, 128), 1) < CAP

    def pairs(part):
        even = meta_ref[pl.ds(part, PAIRS, stride=16), :]
        odd = meta_ref[pl.ds(part + 8, PAIRS, stride=16), :]
        return jnp.where(first, even, odd).astype(jnp.int32) - 1

    x, y, z = pairs(0), pairs(1), pairs(2)
    live = x >= 0
    x = x ^ (half_ref[0] * (BX // 2))
    labels_ref[0] = jnp.where(live, x * 16 + (z & 15), -1)
    labels_ref[1] = jnp.where(live, x * 8 + (y & 7), -1)
    labels_ref[2] = jnp.where(live, y * 32 + z, -1)
    labels_ref[3] = (y >> 3) & 1
    labels_ref[4] = (z >> 4) & 1

    points = got_ref[:, 0:CAP, :].reshape(SLOTS, C)
    for block in range(2):
        sums = jnp.dot(onehot(labels_ref.at[2], block * 256, 256, PAIRS), points, preferred_element_type=F32)
        side_ref[block * 8 : block * 8 + 8] = sums.reshape(8, NZ, C)


def split_points(got_ref, half_ref, rhs_ref):
    for q in range(PAIRS):
        piece = got_ref[q * 2 : q * 2 + 2, 0:CAP, :].reshape(128, C)
        half = columns_of(half_ref[pl.ds(q, 1), :].astype(F32))
        rhs_ref[q * 128 : (q + 1) * 128, :] = split_columns(piece, half)


def pool_front_kernel(got_ref, labels_ref, mine_ref, other_ref, rhs_ref):
    split_points(got_ref, labels_ref.at[4], rhs_ref)
    for block in range(4):
        sums = jnp.dot(onehot(labels_ref.at[0], block * 256, 256, PAIRS), rhs_ref[...], preferred_element_type=F32)
        out = (mine_ref, other_ref)[block // 2]
        xs = pl.ds(block % 2 * 16, 16)
        out[xs, 0:16, :] = sums[:, :C].reshape(16, 16, C)
        out[xs, 16:32, :] = sums[:, C:].reshape(16, 16, C)


def pool_top_kernel(got_ref, labels_ref, top_ref, rhs_ref):
    split_points(got_ref, labels_ref.at[3], rhs_ref)
    for block in range(2):
        sums = jnp.dot(onehot(labels_ref.at[1], block * 256, 256, PAIRS), rhs_ref[...], preferred_element_type=F32)
        xs = pl.ds(block * 32, 32)
        top_ref[xs, 0:8, :] = sums[:, :C].reshape(32, 8, C)
        top_ref[xs, 8:16, :] = sums[:, C:].reshape(32, 8, C)


def call(kernel, ins, outs, scratch, flops, name):
    whole = pl.BlockSpec(memory_space=pltpu.VMEM)
    small = pl.BlockSpec(memory_space=pltpu.SMEM)
    return pl.pallas_call(
        kernel,
        out_shape=outs,
        in_specs=[small if i.dtype == jnp.int32 and i.size == 1 else whole for i in ins],
        out_specs=[whole] * len(outs),
        scratch_shapes=scratch,
        compiler_params=pltpu.CompilerParams(vmem_limit_bytes=VMEM_LIMIT),
        cost_estimate=pl.CostEstimate(flops=flops, bytes_accessed=4 * 2**20, transcendentals=0),
        name=name,
    )(*ins)


def pool_side(half, got):
    return call(
        pool_side_kernel,
        [half, got],
        [jax.ShapeDtypeStruct((BY, NZ, C), F32), jax.ShapeDtypeStruct((5, PAIRS, 128), jnp.int32)],
        [pltpu.VMEM((DEVICES * 8, 128), F32)],
        2 * 8192 * 512 * 256,
        "pool_side",
    )


def pool_front(got, labels):
    shape = jax.ShapeDtypeStruct((BX // 2, NZ, C), F32)
    scratch = [pltpu.VMEM((SLOTS, 2 * C), BF16)]
    return call(pool_front_kernel, [got, labels], [shape, shape], scratch, 2 * 8192 * 1024 * 256 * 2, "pool_front")


def pool_top(got, labels):
    return call(
        pool_top_kernel,
        [got, labels],
        [jax.ShapeDtypeStruct((BX, BY, C), F32)],
        [pltpu.VMEM((SLOTS, 2 * C), BF16)],
        2 * 8192 * 768 * 256 * 2,
        "pool_top",
    )[0]


def gelu(x):
    half = 0.5 * x
    return half + half * lax.erf(x * 0.7071067811865476)


STEP = 4


def mlp_kernel(half_ref, top_ref, mine_ref, other_ref, side_ref, w_in_ref, b_in_ref, w_out_ref, b_out_ref, out_ref):
    def work(front_ref):
        for i in range(STEP):
            top = top_ref[i].astype(BF16).astype(F32)
            front = front_ref[i].astype(F32)
            cell = (top[:, None, :] + front[None, :, :] + side_ref[...].astype(F32)).astype(BF16)
            cell = cell.reshape(BY * NZ, C)
            hidden = jnp.dot(cell, w_in_ref[...], preferred_element_type=F32) + b_in_ref[...]
            hidden = gelu(hidden).astype(BF16)
            result = jnp.dot(hidden, w_out_ref[...], preferred_element_type=F32)
            result = result + b_out_ref[...] + cell.astype(F32)
            out_ref[i] = result.astype(BF16).reshape(BY, NZ, C)

    mine = pl.program_id(0) < HALF_STEPS
    pl.when(mine)(lambda: work(mine_ref))
    pl.when(jnp.logical_not(mine))(lambda: work(other_ref))


HALF_STEPS = BX // STEP // 2


def mlp(half, top, mine, other, side, w_in, b_in, w_out, b_out):
    def same(*shape):
        return pl.BlockSpec(shape, lambda i, h: (0,) * len(shape))

    return pl.pallas_call(
        mlp_kernel,
        grid_spec=pltpu.PrefetchScalarGridSpec(
            num_scalar_prefetch=1,
            grid=(BX // STEP,),
            in_specs=[
                pl.BlockSpec((STEP, BY, C), lambda i, h: (i, 0, 0)),
                pl.BlockSpec((STEP, NZ, C), lambda i, h: (jnp.minimum(i, HALF_STEPS - 1), 0, 0)),
                pl.BlockSpec((STEP, NZ, C), lambda i, h: (jnp.maximum(i - HALF_STEPS, 0), 0, 0)),
                same(BY, NZ, C),
                same(C, HID),
                same(1, HID),
                same(HID, C),
                same(1, C),
            ],
            out_specs=pl.BlockSpec((STEP, BY, NZ, C), lambda i, h: (i ^ (h[0] * HALF_STEPS), 0, 0, 0)),
        ),
        out_shape=jax.ShapeDtypeStruct((BX, BY, NZ, C), BF16),
        compiler_params=pltpu.CompilerParams(vmem_limit_bytes=VMEM_LIMIT),
        cost_estimate=pl.CostEstimate(
            flops=4 * BX * BY * NZ * C * HID, bytes_accessed=9 * 2**20, transcendentals=BX * BY * NZ * HID
        ),
        name="voxel_mlp",
    )(half, top, mine, other, side, w_in, b_in.reshape(1, HID), w_out, b_out.reshape(1, C))


SAME_CORE = [list(range(core, N_GY, 2)) for core in range(2)]
OTHER_CORE = [(i, i ^ 1) for i in range(N_GY)]


def plane_sum(part, axis, groups=None):
    rows = part.shape[0] * part.shape[1] // 8
    pieces = lax.all_to_all(part.reshape(8, rows, C), axis, 0, 0, tiled=True, axis_index_groups=groups)
    share = jnp.sum(pieces, axis=0).astype(BF16)
    copies = jnp.broadcast_to(share[None], (8, rows, C))
    whole = lax.all_to_all(copies, axis, 0, 0, tiled=True, axis_index_groups=groups)
    return whole.reshape(part.shape)


def per_device(
    point_feats, top_bin, front_bin, side_bin, camera_of_device, camera_embed, w_in, b_in, w_out, b_out
):
    half = (lax.axis_index("gy") & 1).astype(jnp.int32).reshape(1)
    sent = pack(camera_of_device, point_feats, top_bin, front_bin, camera_embed)
    got = lax.all_to_all(sent, ("gx", "gy"), split_axis=0, concat_axis=0, tiled=True)
    side_part, labels = pool_side(half, got)
    side = plane_sum(side_part, "gx")
    mine, other = pool_front(got, labels)
    mine = mine + lax.ppermute(other, "gy", OTHER_CORE)
    top = pool_top(got, labels)
    mine, top, side = lax.optimization_barrier((mine, top, side))
    mine = plane_sum(mine, "gy", SAME_CORE)
    other = lax.ppermute(mine, "gy", OTHER_CORE)
    return mlp(half, top, mine, other, side, w_in, b_in, w_out, b_out)


def solution(mesh):
    points = P(("gx", "gy"))
    placed = (P(("gx", "gy"), None), points, points, points, points, P(), P(), P(), P(), P())
    return jax.shard_map(
        per_device, mesh=mesh, in_specs=placed, out_specs=P("gx", "gy", None, None), check_vma=False
    )
```

```python
import jax
import jax.numpy as jnp
from jax import lax
from jax.experimental import pallas as pl
from jax.experimental.pallas import tpu as pltpu
from jax.sharding import PartitionSpec as P

C = 128
HID = 256
CAMS = 6
NZ = 32
BX = 64
BY = 16
P_DEV = 4096
DEVICES = 128
N_GX = 8
N_GY = 16
CAP = 64
ROWS = CAP + 8
SLOTS = DEVICES * CAP
CHUNKS = P_DEV // 128
PAIRS = DEVICES // 2

F32 = jnp.float32
BF16 = jnp.bfloat16
VMEM_LIMIT = 24 * 2**20
PACK_LIMIT = 60 * 2**20


def iota(shape, axis):
    return lax.broadcasted_iota(jnp.int32, shape, axis)


def columns_of(row):
    diagonal = jnp.where(iota((128, 128), 0) == iota((128, 128), 1), row, 0.0).astype(BF16)
    return jnp.dot(diagonal, jnp.ones((128, 128), BF16), preferred_element_type=F32).astype(BF16)


def split_columns(values, half):
    zero = jnp.zeros_like(values)
    left = half == jnp.zeros_like(half)
    return jnp.concatenate([jnp.where(left, values, zero), jnp.where(left, zero, values)], axis=1)


def onehot_rows(label, base, rows):
    return jnp.where(iota((rows, 128), 0) + base == label, 1.0, 0.0).astype(BF16)


def onehot(labels_ref, base, rows, chunks):
    return jnp.concatenate(
        [onehot_rows(labels_ref[pl.ds(k, 1), :], base, rows) for k in range(chunks)], axis=1
    )


def pack_kernel(
    cam_ref, feats_hbm, top_hbm, front_hbm, embed_hbm, out_hbm,
    feats_ref, top_ref, front_ref, embed_ref, out_ref,
    marks_ref, rank_ref, place_ref, half_ref, rhs_ref, values_ref, sorted_ref, meta_ref, start_ref, start_smem, sems,
):
    loads = [
        pltpu.make_async_copy(source, target, sems.at[i])
        for i, (source, target) in enumerate(
            [(top_hbm, top_ref), (front_hbm, front_ref), (embed_hbm, embed_ref), (feats_hbm, feats_ref)]
        )
    ]
    for load in loads:
        load.start()
    loads[0].wait()
    loads[1].wait()
    top = top_ref[...]
    live = top >= 0
    grid_x = top >> 8
    grid_y = top & 255
    owner = jnp.where(live, (grid_x >> 6) * N_GY + (grid_y >> 4), -1)
    cells = (
        (grid_x & (BX - 1)) + 1,
        (grid_y & (BY - 1)) + 1,
        (front_ref[...] & (NZ - 1)) + 1,
    )
    cells = [cell.astype(F32) for cell in cells]

    for k in range(CHUNKS):
        marks_ref[:, k * 128 : (k + 1) * 128] = onehot_rows(owner[k : k + 1, :], 0, DEVICES)
    totals = jnp.dot(marks_ref[...], jnp.ones((P_DEV, 128), BF16), preferred_element_type=F32)
    below = jnp.where(iota((128, 128), 1) < iota((128, 128), 0), 1.0, 0.0).astype(BF16)
    starts = jnp.dot(below, totals.astype(BF16), preferred_element_type=F32)
    start_row = jnp.sum(
        jnp.where(iota((128, 128), 0) == iota((128, 128), 1), starts, 0.0), axis=0, keepdims=True
    )
    start_ref[...] = start_row.astype(jnp.int32)
    copy = pltpu.make_async_copy(start_ref, start_smem, sems.at[4])
    copy.start()

    before = iota((128, 256), 0) < iota((128, 256), 1)
    later = iota((128, 256), 1) >= 128
    counter = jnp.where(before | later, 1.0, 0.0).astype(BF16)
    seen = jnp.zeros((DEVICES, 128), F32)
    slot = iota((128, 128), 0) & (CAP - 1)
    for k in range(CHUNKS):
        columns = slice(k * 128, (k + 1) * 128)
        mine = iota((DEVICES, 128), 0) == owner[k : k + 1, :]
        counts = jnp.dot(marks_ref[:, columns], counter, preferred_element_type=F32)
        rank = jnp.sum(jnp.where(mine, counts[:, :128] + seen, 0.0), axis=0, keepdims=True)
        start = jnp.sum(jnp.where(mine, starts, 0.0), axis=0, keepdims=True)
        seen = seen + counts[:, 128:]
        place_ref[pl.ds(k, 1), :] = rank + start
        here = slot == rank.astype(jnp.int32)
        for part in range(3):
            values_ref[part * 128 : (part + 1) * 128, columns] = jnp.where(
                here, cells[part][k : k + 1, :], 0.0
            ).astype(BF16)
    place = place_ref[...].astype(jnp.int32)
    half_ref[...] = (place >> 11).astype(F32)
    place_ref[...] = jnp.where(live, place & 2047, -1).astype(F32)

    loads[2].wait()
    loads[3].wait()
    camera = embed_ref[pl.ds(cam_ref[0], 1), :]
    for k in range(CHUNKS):
        rows = slice(k * 128, (k + 1) * 128)
        features = (feats_ref[rows, :].astype(F32) + camera).astype(BF16)
        rhs_ref[rows, :] = split_columns(features, columns_of(half_ref[pl.ds(k, 1), :]))

    rank_ref[...] = place_ref[...].astype(jnp.int32)
    for block in range(8):
        base = block * 256
        picked = jnp.dot(onehot(rank_ref, base, 256, CHUNKS), rhs_ref[...], preferred_element_type=F32)
        sorted_ref[base : base + 256, :] = picked[:, :C]
        sorted_ref[2048 + base : 2304 + base, :] = picked[:, C:]
    sorted_ref[P_DEV : P_DEV + CAP, :] = jnp.zeros((CAP, C), F32)

    meta = lax.dot_general(
        values_ref[...], marks_ref[...], (((1,), (1,)), ((), ())), preferred_element_type=F32
    )
    for part in range(3):
        meta_ref[pl.ds(part, DEVICES, stride=8), :] = meta[part * 128 : (part + 1) * 128, :].T
    for part in range(3, 8):
        meta_ref[pl.ds(part, DEVICES, stride=8), :] = jnp.zeros((DEVICES, 128), F32)
    out_ref[:, CAP:ROWS, :] = meta_ref[...].reshape(DEVICES, 8, 128).astype(BF16)

    copy.wait()

    stores = []
    for part in range(4):

        @pl.loop(0, DEVICES // 4, unroll=8)
        def _(i):
            device = part * (DEVICES // 4) + i
            out_ref[device, 0:CAP, :] = sorted_ref[pl.ds(start_smem[0, device], CAP), :].astype(BF16)

        here = pl.ds(part * (DEVICES // 4), DEVICES // 4)
        stores.append(pltpu.make_async_copy(out_ref.at[here], out_hbm.at[here], sems.at[5 + part]))
        stores[-1].start()
    for store in stores:
        store.wait()


def pack(camera, point_feats, top_bin, front_bin, camera_embed):
    whole = pl.BlockSpec(memory_space=pltpu.HBM)
    return pl.pallas_call(
        pack_kernel,
        out_shape=jax.ShapeDtypeStruct((DEVICES, ROWS, C), BF16),
        in_specs=[pl.BlockSpec(memory_space=pltpu.SMEM)] + [whole] * 4,
        out_specs=whole,
        scratch_shapes=[
            pltpu.VMEM((P_DEV, C), BF16),
            pltpu.VMEM((CHUNKS, 128), jnp.int32),
            pltpu.VMEM((CHUNKS, 128), jnp.int32),
            pltpu.VMEM((CAMS, C), F32),
            pltpu.VMEM((DEVICES, ROWS, C), BF16),
            pltpu.VMEM((DEVICES, P_DEV), BF16),
            pltpu.VMEM((CHUNKS, 128), jnp.int32),
            pltpu.VMEM((CHUNKS, 128), F32),
            pltpu.VMEM((CHUNKS, 128), F32),
            pltpu.VMEM((P_DEV, 2 * C), BF16),
            pltpu.VMEM((3 * 128, P_DEV), BF16),
            pltpu.VMEM((P_DEV + CAP, C), F32),
            pltpu.VMEM((DEVICES * 8, 128), F32),
            pltpu.VMEM((1, DEVICES), jnp.int32),
            pltpu.SMEM((1, DEVICES), jnp.int32),
            pltpu.SemaphoreType.DMA((9,)),
        ],
        compiler_params=pltpu.CompilerParams(vmem_limit_bytes=PACK_LIMIT),
        cost_estimate=pl.CostEstimate(flops=2 * 4096 * 4096 * 256, bytes_accessed=4 * 2**20, transcendentals=0),
        name="pack",
    )(camera, point_feats, top_bin.reshape(CHUNKS, 128), front_bin.reshape(CHUNKS, 128), camera_embed)


def split_points(got_ref, half_ref, rhs_ref):
    for q in range(PAIRS):
        piece = got_ref[q * 2 : q * 2 + 2, 0:CAP, :].reshape(128, C)
        half = columns_of(half_ref[pl.ds(q, 1), :].astype(F32))
        rhs_ref[q * 128 : (q + 1) * 128, :] = split_columns(piece, half)


def pool_front_kernel(place_ref, got_ref, mine_ref, other_ref, labels_ref, meta_ref, rhs_ref):
    meta_ref[...] = got_ref[:, CAP:ROWS, :].astype(F32).reshape(DEVICES * 8, 128)
    first = iota((PAIRS, 128), 1) < CAP

    def pairs(part):
        even = meta_ref[pl.ds(part, PAIRS, stride=16), :]
        odd = meta_ref[pl.ds(part + 8, PAIRS, stride=16), :]
        return jnp.where(first, even, odd).astype(jnp.int32) - 1

    x, y, z = pairs(0), pairs(1), pairs(2)
    live = x >= 0
    x = x ^ (place_ref[0] * (BX // 2))
    labels_ref[0] = jnp.where(live, x * 16 + (z & 15), -1)
    labels_ref[1] = jnp.where(live, x * 8 + (y & 7), -1)
    labels_ref[2] = jnp.where(live, (y ^ place_ref[1]) * 32 + z, -1)
    labels_ref[3] = (y >> 3) & 1
    labels_ref[4] = (z >> 4) & 1
    split_points(got_ref, labels_ref.at[4], rhs_ref)
    for block in range(4):
        sums = jnp.dot(onehot(labels_ref.at[0], block * 256, 256, PAIRS), rhs_ref[...], preferred_element_type=F32)
        out = (mine_ref, other_ref)[block // 2]
        xs = pl.ds(block % 2 * 16, 16)
        out[xs, 0:16, :] = sums[:, :C].reshape(16, 16, C)
        out[xs, 16:32, :] = sums[:, C:].reshape(16, 16, C)


def pool_side_kernel(got_ref, labels_ref, keep_ref, send_ref):
    points = got_ref[:, 0:CAP, :].reshape(SLOTS, C)
    for block, out in enumerate((keep_ref, send_ref)):
        sums = jnp.dot(onehot(labels_ref.at[2], block * 256, 256, PAIRS), points, preferred_element_type=F32)
        out[...] = sums.reshape(BY // 2, NZ, C)


def pool_top_kernel(got_ref, labels_ref, top_ref, rhs_ref):
    split_points(got_ref, labels_ref.at[3], rhs_ref)
    for block in range(2):
        sums = jnp.dot(onehot(labels_ref.at[1], block * 256, 256, PAIRS), rhs_ref[...], preferred_element_type=F32)
        xs = pl.ds(block * 32, 32)
        top_ref[xs, 0:8, :] = sums[:, :C].reshape(32, 8, C)
        top_ref[xs, 8:16, :] = sums[:, C:].reshape(32, 8, C)


def call(kernel, ins, outs, scratch, flops, name):
    whole = pl.BlockSpec(memory_space=pltpu.VMEM)
    small = pl.BlockSpec(memory_space=pltpu.SMEM)
    return pl.pallas_call(
        kernel,
        out_shape=outs,
        in_specs=[small if i.dtype == jnp.int32 and i.size == 2 else whole for i in ins],
        out_specs=[whole] * len(outs),
        scratch_shapes=scratch,
        compiler_params=pltpu.CompilerParams(vmem_limit_bytes=VMEM_LIMIT),
        cost_estimate=pl.CostEstimate(flops=flops, bytes_accessed=4 * 2**20, transcendentals=0),
        name=name,
    )(*ins)


def pool_front(place, got):
    shape = jax.ShapeDtypeStruct((BX // 2, NZ, C), F32)
    return call(
        pool_front_kernel,
        [place, got],
        [shape, shape, jax.ShapeDtypeStruct((5, PAIRS, 128), jnp.int32)],
        [pltpu.VMEM((DEVICES * 8, 128), F32), pltpu.VMEM((SLOTS, 2 * C), BF16)],
        2 * 8192 * 1024 * 256 * 2,
        "pool_front",
    )


def pool_side(got, labels):
    shape = jax.ShapeDtypeStruct((BY // 2, NZ, C), F32)
    return call(pool_side_kernel, [got, labels], [shape, shape], [], 2 * 8192 * 512 * 256, "pool_side")


def fold_kernel(keep_ref, got_ref, *out_refs):
    for k, out in enumerate(out_refs):
        rows = pl.ds(k * 2, 2)
        out[...] = keep_ref[rows] + got_ref[rows]


def fold(keep, got):
    shape = jax.ShapeDtypeStruct((2, NZ, C), F32)
    return call(fold_kernel, [keep, got], [shape] * 4, [], 1024, "fold")


def pool_top(got, labels):
    return call(
        pool_top_kernel,
        [got, labels],
        [jax.ShapeDtypeStruct((BX, BY, C), F32)],
        [pltpu.VMEM((SLOTS, 2 * C), BF16)],
        2 * 8192 * 768 * 256 * 2,
        "pool_top",
    )[0]


def gelu(x):
    half = 0.5 * x
    return half + half * lax.erf(x * 0.7071067811865476)


STEP = 4


def mlp_kernel(
    place_ref, top_ref, mine_ref, other_ref, near_ref, far_ref, w_in_ref, b_in_ref, w_out_ref, b_out_ref, out_ref, side_ref
):
    @pl.when(pl.program_id(0) == 0)
    def _():
        for y in range(BY // 2):
            side_ref[y ^ place_ref[1]] = near_ref[y]
            side_ref[(y + BY // 2) ^ place_ref[1]] = far_ref[y]

    def work(front_ref):
        for i in range(STEP):
            top = top_ref[i].astype(BF16).astype(F32)
            front = front_ref[i].astype(F32)
            cell = (top[:, None, :] + front[None, :, :] + side_ref[...].astype(F32)).astype(BF16)
            cell = cell.reshape(BY * NZ, C)
            hidden = jnp.dot(cell, w_in_ref[...], preferred_element_type=F32) + b_in_ref[...]
            hidden = gelu(hidden).astype(BF16)
            result = jnp.dot(hidden, w_out_ref[...], preferred_element_type=F32)
            result = result + b_out_ref[...] + cell.astype(F32)
            out_ref[i] = result.astype(BF16).reshape(BY, NZ, C)

    mine = pl.program_id(0) < HALF_STEPS
    pl.when(mine)(lambda: work(mine_ref))
    pl.when(jnp.logical_not(mine))(lambda: work(other_ref))


HALF_STEPS = BX // STEP // 2


def mlp(place, top, mine, other, near, far, w_in, b_in, w_out, b_out):
    def same(*shape):
        return pl.BlockSpec(shape, lambda i, h: (0,) * len(shape))

    return pl.pallas_call(
        mlp_kernel,
        grid_spec=pltpu.PrefetchScalarGridSpec(
            num_scalar_prefetch=1,
            grid=(BX // STEP,),
            in_specs=[
                pl.BlockSpec((STEP, BY, C), lambda i, h: (i, 0, 0)),
                pl.BlockSpec((STEP, NZ, C), lambda i, h: (jnp.minimum(i, HALF_STEPS - 1), 0, 0)),
                pl.BlockSpec((STEP, NZ, C), lambda i, h: (jnp.maximum(i - HALF_STEPS, 0), 0, 0)),
                same(BY // 2, NZ, C),
                same(BY // 2, NZ, C),
                same(C, HID),
                same(1, HID),
                same(HID, C),
                same(1, C),
            ],
            out_specs=pl.BlockSpec((STEP, BY, NZ, C), lambda i, h: (i ^ (h[0] * HALF_STEPS), 0, 0, 0)),
            scratch_shapes=[pltpu.VMEM((BY, NZ, C), BF16)],
        ),
        out_shape=jax.ShapeDtypeStruct((BX, BY, NZ, C), BF16),
        compiler_params=pltpu.CompilerParams(vmem_limit_bytes=VMEM_LIMIT),
        cost_estimate=pl.CostEstimate(
            flops=4 * BX * BY * NZ * C * HID, bytes_accessed=9 * 2**20, transcendentals=BX * BY * NZ * HID
        ),
        name="voxel_mlp",
    )(place, top, mine, other, near, far, w_in, b_in.reshape(1, HID), w_out, b_out.reshape(1, C))


SAME_CORE = [list(range(core, N_GY, 2)) for core in range(2)]


def swap(array, axis, size, bit):
    return lax.ppermute(array, axis, [(i, i ^ bit) for i in range(size)])


def front_share(mine):
    pieces = mine.reshape(8, mine.shape[0] * mine.shape[1] // 8, C)
    pieces = lax.all_to_all(pieces, "gy", 0, 0, tiled=True, axis_index_groups=SAME_CORE)
    return jnp.sum(pieces, axis=0).astype(BF16)


def front_gather(share):
    copies = jnp.broadcast_to(share[None], (8,) + share.shape)
    whole = lax.all_to_all(copies, "gy", 0, 0, tiled=True, axis_index_groups=SAME_CORE)
    return whole.reshape(BX // 2, NZ, C)


def side_share(keep, send):
    parts = fold(keep, swap(send, "gx", N_GX, 4))
    return (
        parts[0] + swap(parts[1], "gx", N_GX, 2) + swap(parts[2], "gx", N_GX, 1) + swap(parts[3], "gx", N_GX, 3)
    ).astype(BF16)


def side_gather(share):
    near = jnp.concatenate([share] + [swap(share, "gx", N_GX, bit) for bit in (2, 1, 3)], axis=0)
    return near, swap(near, "gx", N_GX, 4)


def per_device(
    point_feats, top_bin, front_bin, side_bin, camera_of_device, camera_embed, w_in, b_in, w_out, b_out
):
    row = lax.axis_index("gx")
    place = jnp.stack(
        [lax.axis_index("gy") & 1, (row >> 2 & 1) * 8 + (row & 1) * 4 + (row >> 1 & 1) * 2]
    ).astype(jnp.int32)
    sent = pack(camera_of_device, point_feats, top_bin, front_bin, camera_embed)
    got = lax.all_to_all(sent, ("gx", "gy"), split_axis=0, concat_axis=0, tiled=True)
    mine, other, labels = pool_front(place, got)
    keep, send = pool_side(got, labels)
    mine = mine + swap(other, "gy", N_GY, 1)
    mine, keep, send = lax.optimization_barrier((mine, keep, send))
    top = pool_top(got, labels)
    shares = (front_share(mine), side_share(keep, send), top)
    front, side, top = lax.optimization_barrier(shares)
    mine = front_gather(front)
    near, far = side_gather(side)
    other = swap(mine, "gy", N_GY, 1)
    return mlp(place, top, mine, other, near, far, w_in, b_in, w_out, b_out)


def solution(mesh):
    points = P(("gx", "gy"))
    placed = (P(("gx", "gy"), None), points, points, points, points, P(), P(), P(), P(), P())
    return jax.shard_map(
        per_device, mesh=mesh, in_specs=placed, out_specs=P("gx", "gy", None, None), check_vma=False
    )
```

```python
import jax
import jax.numpy as jnp
from jax import lax
from jax.experimental import pallas as pl
from jax.experimental.pallas import tpu as pltpu
from jax.sharding import PartitionSpec as P

C = 128
HID = 256
CAMS = 6
NZ = 32
BX = 64
BY = 16
P_DEV = 4096
DEVICES = 128
N_GX = 8
N_GY = 16
CAP = 64
ROWS = CAP + 8
SLOTS = DEVICES * CAP
CHUNKS = P_DEV // 128
PAIRS = DEVICES // 2

F32 = jnp.float32
BF16 = jnp.bfloat16
VMEM_LIMIT = 24 * 2**20
PACK_LIMIT = 60 * 2**20
MLP_LIMIT = 40 * 2**20


def iota(shape, axis):
    return lax.broadcasted_iota(jnp.int32, shape, axis)


def columns_of(row):
    diagonal = jnp.where(iota((128, 128), 0) == iota((128, 128), 1), row, 0.0).astype(BF16)
    return jnp.dot(diagonal, jnp.ones((128, 128), BF16), preferred_element_type=F32).astype(BF16)


def split_columns(values, half):
    zero = jnp.zeros_like(values)
    left = half == jnp.zeros_like(half)
    return jnp.concatenate([jnp.where(left, values, zero), jnp.where(left, zero, values)], axis=1)


def onehot_rows(label, base, rows):
    return jnp.where(iota((rows, 128), 0) + base == label, 1.0, 0.0).astype(BF16)


def onehot(labels_ref, base, rows, chunks):
    return jnp.concatenate(
        [onehot_rows(labels_ref[pl.ds(k, 1), :], base, rows) for k in range(chunks)], axis=1
    )


def pack_kernel(
    cam_ref, feats_hbm, top_hbm, front_hbm, embed_hbm, out_hbm,
    feats_ref, top_ref, front_ref, embed_ref, out_ref,
    marks_ref, rank_ref, place_ref, half_ref, rhs_ref, values_ref, sorted_ref, meta_ref, start_ref, start_smem, sems,
):
    loads = [
        pltpu.make_async_copy(source, target, sems.at[i])
        for i, (source, target) in enumerate(
            [(top_hbm, top_ref), (front_hbm, front_ref), (embed_hbm, embed_ref), (feats_hbm, feats_ref)]
        )
    ]
    for load in loads:
        load.start()
    loads[0].wait()
    loads[1].wait()
    top = top_ref[...]
    live = top >= 0
    grid_x = top >> 8
    grid_y = top & 255
    owner = jnp.where(live, (grid_x >> 6) * N_GY + (grid_y >> 4), -1)
    cells = (
        (grid_x & (BX - 1)) + 1,
        (grid_y & (BY - 1)) + 1,
        (front_ref[...] & (NZ - 1)) + 1,
    )
    cells = [cell.astype(F32) for cell in cells]

    for k in range(CHUNKS):
        marks_ref[:, k * 128 : (k + 1) * 128] = onehot_rows(owner[k : k + 1, :], 0, DEVICES)
    totals = jnp.dot(marks_ref[...], jnp.ones((P_DEV, 128), BF16), preferred_element_type=F32)
    below = jnp.where(iota((128, 128), 1) < iota((128, 128), 0), 1.0, 0.0).astype(BF16)
    starts = jnp.dot(below, totals.astype(BF16), preferred_element_type=F32)
    start_row = jnp.sum(
        jnp.where(iota((128, 128), 0) == iota((128, 128), 1), starts, 0.0), axis=0, keepdims=True
    )
    start_ref[...] = start_row.astype(jnp.int32)
    copy = pltpu.make_async_copy(start_ref, start_smem, sems.at[4])
    copy.start()

    before = iota((128, 256), 0) < iota((128, 256), 1)
    later = iota((128, 256), 1) >= 128
    counter = jnp.where(before | later, 1.0, 0.0).astype(BF16)
    seen = jnp.zeros((DEVICES, 128), F32)
    slot = iota((128, 128), 0) & (CAP - 1)
    for k in range(CHUNKS):
        columns = slice(k * 128, (k + 1) * 128)
        mine = iota((DEVICES, 128), 0) == owner[k : k + 1, :]
        counts = jnp.dot(marks_ref[:, columns], counter, preferred_element_type=F32)
        rank = jnp.sum(jnp.where(mine, counts[:, :128] + seen, 0.0), axis=0, keepdims=True)
        start = jnp.sum(jnp.where(mine, starts, 0.0), axis=0, keepdims=True)
        seen = seen + counts[:, 128:]
        place_ref[pl.ds(k, 1), :] = rank + start
        here = slot == rank.astype(jnp.int32)
        for part in range(3):
            values_ref[part * 128 : (part + 1) * 128, columns] = jnp.where(
                here, cells[part][k : k + 1, :], 0.0
            ).astype(BF16)
    place = place_ref[...].astype(jnp.int32)
    half_ref[...] = (place >> 11).astype(F32)
    place_ref[...] = jnp.where(live, place & 2047, -1).astype(F32)

    loads[2].wait()
    loads[3].wait()
    camera = embed_ref[pl.ds(cam_ref[0], 1), :]
    for k in range(CHUNKS):
        rows = slice(k * 128, (k + 1) * 128)
        features = (feats_ref[rows, :].astype(F32) + camera).astype(BF16)
        rhs_ref[rows, :] = split_columns(features, columns_of(half_ref[pl.ds(k, 1), :]))

    rank_ref[...] = place_ref[...].astype(jnp.int32)
    for block in range(8):
        base = block * 256
        picked = jnp.dot(onehot(rank_ref, base, 256, CHUNKS), rhs_ref[...], preferred_element_type=F32)
        sorted_ref[base : base + 256, :] = picked[:, :C]
        sorted_ref[2048 + base : 2304 + base, :] = picked[:, C:]
    sorted_ref[P_DEV : P_DEV + CAP, :] = jnp.zeros((CAP, C), F32)

    meta = lax.dot_general(
        values_ref[...], marks_ref[...], (((1,), (1,)), ((), ())), preferred_element_type=F32
    )
    for part in range(3):
        meta_ref[pl.ds(part, DEVICES, stride=8), :] = meta[part * 128 : (part + 1) * 128, :].T
    for part in range(3, 8):
        meta_ref[pl.ds(part, DEVICES, stride=8), :] = jnp.zeros((DEVICES, 128), F32)
    out_ref[:, CAP:ROWS, :] = meta_ref[...].reshape(DEVICES, 8, 128).astype(BF16)

    copy.wait()

    stores = []
    for part in range(4):

        @pl.loop(0, DEVICES // 4, unroll=8)
        def _(i):
            device = part * (DEVICES // 4) + i
            out_ref[device, 0:CAP, :] = sorted_ref[pl.ds(start_smem[0, device], CAP), :].astype(BF16)

        here = pl.ds(part * (DEVICES // 4), DEVICES // 4)
        stores.append(pltpu.make_async_copy(out_ref.at[here], out_hbm.at[here], sems.at[5 + part]))
        stores[-1].start()
    for store in stores:
        store.wait()


def pack(camera, point_feats, top_bin, front_bin, camera_embed):
    whole = pl.BlockSpec(memory_space=pltpu.HBM)
    return pl.pallas_call(
        pack_kernel,
        out_shape=jax.ShapeDtypeStruct((DEVICES, ROWS, C), BF16),
        in_specs=[pl.BlockSpec(memory_space=pltpu.SMEM)] + [whole] * 4,
        out_specs=whole,
        scratch_shapes=[
            pltpu.VMEM((P_DEV, C), BF16),
            pltpu.VMEM((CHUNKS, 128), jnp.int32),
            pltpu.VMEM((CHUNKS, 128), jnp.int32),
            pltpu.VMEM((CAMS, C), F32),
            pltpu.VMEM((DEVICES, ROWS, C), BF16),
            pltpu.VMEM((DEVICES, P_DEV), BF16),
            pltpu.VMEM((CHUNKS, 128), jnp.int32),
            pltpu.VMEM((CHUNKS, 128), F32),
            pltpu.VMEM((CHUNKS, 128), F32),
            pltpu.VMEM((P_DEV, 2 * C), BF16),
            pltpu.VMEM((3 * 128, P_DEV), BF16),
            pltpu.VMEM((P_DEV + CAP, C), F32),
            pltpu.VMEM((DEVICES * 8, 128), F32),
            pltpu.VMEM((1, DEVICES), jnp.int32),
            pltpu.SMEM((1, DEVICES), jnp.int32),
            pltpu.SemaphoreType.DMA((9,)),
        ],
        compiler_params=pltpu.CompilerParams(vmem_limit_bytes=PACK_LIMIT),
        cost_estimate=pl.CostEstimate(flops=2 * 4096 * 4096 * 256, bytes_accessed=4 * 2**20, transcendentals=0),
        name="pack",
    )(camera, point_feats, top_bin.reshape(CHUNKS, 128), front_bin.reshape(CHUNKS, 128), camera_embed)


def split_points(got_ref, half_ref, rhs_ref):
    for q in range(PAIRS):
        piece = got_ref[q * 2 : q * 2 + 2, 0:CAP, :].reshape(128, C)
        half = columns_of(half_ref[pl.ds(q, 1), :].astype(F32))
        rhs_ref[q * 128 : (q + 1) * 128, :] = split_columns(piece, half)


def pool_front_kernel(place_ref, got_ref, mine_ref, other_ref, labels_ref, meta_ref, rhs_ref):
    meta_ref[...] = got_ref[:, CAP:ROWS, :].astype(F32).reshape(DEVICES * 8, 128)
    first = iota((PAIRS, 128), 1) < CAP

    def pairs(part):
        even = meta_ref[pl.ds(part, PAIRS, stride=16), :]
        odd = meta_ref[pl.ds(part + 8, PAIRS, stride=16), :]
        return jnp.where(first, even, odd).astype(jnp.int32) - 1

    x, y, z = pairs(0), pairs(1), pairs(2)
    live = x >= 0
    x = x ^ (place_ref[0] * (BX // 2))
    labels_ref[0] = jnp.where(live, x * 16 + (z & 15), -1)
    labels_ref[1] = jnp.where(live, x * 8 + (y & 7), -1)
    labels_ref[2] = jnp.where(live, (y ^ place_ref[1]) * 32 + z, -1)
    labels_ref[3] = (y >> 3) & 1
    labels_ref[4] = (z >> 4) & 1
    split_points(got_ref, labels_ref.at[4], rhs_ref)
    for block in range(4):
        sums = jnp.dot(onehot(labels_ref.at[0], block * 256, 256, PAIRS), rhs_ref[...], preferred_element_type=F32)
        out = (mine_ref, other_ref)[block // 2]
        xs = pl.ds(block % 2 * 16, 16)
        out[xs, 0:16, :] = sums[:, :C].reshape(16, 16, C)
        out[xs, 16:32, :] = sums[:, C:].reshape(16, 16, C)


def pool_side_kernel(got_ref, labels_ref, keep_ref, send_ref):
    points = got_ref[:, 0:CAP, :].reshape(SLOTS, C)
    for block, out in enumerate((keep_ref, send_ref)):
        sums = jnp.dot(onehot(labels_ref.at[2], block * 256, 256, PAIRS), points, preferred_element_type=F32)
        out[...] = sums.reshape(BY // 2, NZ, C)


def pool_top_kernel(got_ref, labels_ref, top_ref, rhs_ref):
    split_points(got_ref, labels_ref.at[3], rhs_ref)
    for block in range(2):
        sums = jnp.dot(onehot(labels_ref.at[1], block * 256, 256, PAIRS), rhs_ref[...], preferred_element_type=F32)
        halves = [sums[:, :C].reshape(32, 8, C), sums[:, C:].reshape(32, 8, C)]
        top_ref[pl.ds(block * 32, 32)] = jnp.concatenate(halves, axis=1).astype(BF16)


def call(kernel, ins, outs, scratch, flops, name):
    whole = pl.BlockSpec(memory_space=pltpu.VMEM)
    small = pl.BlockSpec(memory_space=pltpu.SMEM)
    return pl.pallas_call(
        kernel,
        out_shape=outs,
        in_specs=[small if i.dtype == jnp.int32 and i.size == 2 else whole for i in ins],
        out_specs=[whole] * len(outs),
        scratch_shapes=scratch,
        compiler_params=pltpu.CompilerParams(vmem_limit_bytes=VMEM_LIMIT),
        cost_estimate=pl.CostEstimate(flops=flops, bytes_accessed=flops // 1024, transcendentals=0),
        name=name,
    )(*ins)


def pool_front(place, got):
    shape = jax.ShapeDtypeStruct((BX // 2, NZ, C), F32)
    return call(
        pool_front_kernel,
        [place, got],
        [shape, shape, jax.ShapeDtypeStruct((5, PAIRS, 128), jnp.int32)],
        [pltpu.VMEM((DEVICES * 8, 128), F32), pltpu.VMEM((SLOTS, 2 * C), BF16)],
        2 * 8192 * 1024 * 256 * 2,
        "pool_front",
    )


def pool_side(got, labels):
    shape = jax.ShapeDtypeStruct((BY // 2, NZ, C), F32)
    return call(pool_side_kernel, [got, labels], [shape, shape], [], 2 * 8192 * 512 * 256, "pool_side")


def fold_kernel(keep_ref, got_ref, *out_refs):
    for k, out in enumerate(out_refs):
        rows = pl.ds(k * 2, 2)
        out[...] = keep_ref[rows] + got_ref[rows]


def fold(keep, got):
    shape = jax.ShapeDtypeStruct((2, NZ, C), F32)
    return call(fold_kernel, [keep, got], [shape] * 4, [], 1024, "fold")


def pool_top(got, labels):
    return call(
        pool_top_kernel,
        [got, labels],
        [jax.ShapeDtypeStruct((BX, BY, C), BF16)],
        [pltpu.VMEM((SLOTS, 2 * C), BF16)],
        1024,
        "pool_top",
    )[0]


STEP = 16
HALF_STEPS = BX // STEP // 2


def mlp_kernel(
    place_ref, top_ref, mine_ref, other_ref, s0_ref, s1_ref, s2_ref, s3_ref,
    w_in_ref, b_in_ref, w_out_ref, b_out_ref, out_ref, side_ref, wide_ref, half_ref,
):
    @pl.when(pl.program_id(0) == 0)
    def _():
        for k, rows in enumerate((s0_ref, s1_ref, s2_ref, s3_ref)):
            for j in range(4):
                y = k * 2 + j if j < 2 else BY // 2 + k * 2 + j - 2
                side_ref[y ^ place_ref[1]] = rows[j].astype(F32)
        bias = b_in_ref[...]
        high = bias.astype(BF16).astype(F32)
        middle = (bias - high).astype(BF16).astype(F32)
        low = bias - high - middle
        row = iota((C, HID), 0)
        rest = jnp.where(row == 0, high, jnp.where(row == 1, middle, jnp.where(row == 2, low, 0.0)))
        wide_ref[0:C, :] = w_in_ref[...]
        wide_ref[C : 2 * C, :] = rest.astype(BF16)
        half_ref[...] = (w_out_ref[...].astype(F32) * 0.5).astype(BF16)

    mine = pl.program_id(0) < HALF_STEPS
    ones = jnp.where(iota((BY * NZ, C), 1) < 3, 1.0, 0.0).astype(BF16)
    for i in range(STEP):
        top = top_ref[i].astype(F32)
        front = jnp.where(mine, mine_ref[i].astype(F32), other_ref[i].astype(F32))
        cell = (top[:, None, :] + front[None, :, :] + side_ref[...]).astype(BF16).reshape(BY * NZ, C)
        inner = jnp.dot(jnp.concatenate([cell, ones], axis=1), wide_ref[...], preferred_element_type=F32)
        twice = (inner * (1.0 + lax.erf(inner * 0.7071067811865476))).astype(BF16)
        result = jnp.dot(twice, half_ref[...], preferred_element_type=F32)
        result = result + (b_out_ref[...] + cell.astype(F32))
        out_ref[i] = result.astype(BF16).reshape(BY, NZ, C)


def mlp(place, top, mine, other, sides, w_in, b_in, w_out, b_out):
    def same(*shape):
        return pl.BlockSpec(shape, lambda i, h: (0,) * len(shape))

    return pl.pallas_call(
        mlp_kernel,
        grid_spec=pltpu.PrefetchScalarGridSpec(
            num_scalar_prefetch=1,
            grid=(BX // STEP,),
            in_specs=[
                pl.BlockSpec((STEP, BY, C), lambda i, h: (i, 0, 0)),
                pl.BlockSpec((STEP, NZ, C), lambda i, h: (jnp.minimum(i, HALF_STEPS - 1), 0, 0)),
                pl.BlockSpec((STEP, NZ, C), lambda i, h: (jnp.maximum(i - HALF_STEPS, 0), 0, 0)),
            ]
            + [same(4, NZ, C)] * 4
            + [same(C, HID), same(1, HID), same(HID, C), same(1, C)],
            out_specs=pl.BlockSpec((STEP, BY, NZ, C), lambda i, h: (i ^ (h[0] * HALF_STEPS), 0, 0, 0)),
            scratch_shapes=[
                pltpu.VMEM((BY, NZ, C), F32),
                pltpu.VMEM((2 * C, HID), BF16),
                pltpu.VMEM((HID, C), BF16),
            ],
        ),
        out_shape=jax.ShapeDtypeStruct((BX, BY, NZ, C), BF16),
        compiler_params=pltpu.CompilerParams(vmem_limit_bytes=MLP_LIMIT),
        cost_estimate=pl.CostEstimate(
            flops=4 * BX * BY * NZ * C * HID, bytes_accessed=9 * 2**20, transcendentals=BX * BY * NZ * HID
        ),
        name="voxel_mlp",
    )(place, top, mine, other, *sides, w_in, b_in.reshape(1, HID), w_out, b_out.reshape(1, C))


SAME_CORE = [list(range(core, N_GY, 2)) for core in range(2)]


def swap(array, axis, size, bit):
    return lax.ppermute(array, axis, [(i, i ^ bit) for i in range(size)])


def spread_kernel(pieces_ref, out_ref):
    share = jnp.sum(pieces_ref[...], axis=0).astype(BF16)
    for i in range(8):
        out_ref[i] = share


def front_share(mine):
    pieces = mine.reshape(8, mine.shape[0] * mine.shape[1] // 8, C)
    pieces = lax.all_to_all(pieces, "gy", 0, 0, tiled=True, axis_index_groups=SAME_CORE)
    return call(spread_kernel, [pieces], [jax.ShapeDtypeStruct(pieces.shape, BF16)], [], 1024, "spread")[0]


def front_gather(copies):
    whole = lax.all_to_all(copies, "gy", 0, 0, tiled=True, axis_index_groups=SAME_CORE)
    return whole.reshape(BX // 2, NZ, C)


def side_share(keep, send):
    parts = fold(keep, swap(send, "gx", N_GX, 4))
    share = (
        parts[0] + swap(parts[1], "gx", N_GX, 2) + swap(parts[2], "gx", N_GX, 1) + swap(parts[3], "gx", N_GX, 3)
    ).astype(BF16)
    return jnp.concatenate([share, swap(share, "gx", N_GX, 4)], axis=0)


def side_gather(share):
    return [share] + [swap(share, "gx", N_GX, bit) for bit in (2, 1, 3)]


def per_device(
    point_feats, top_bin, front_bin, side_bin, camera_of_device, camera_embed, w_in, b_in, w_out, b_out
):
    row = lax.axis_index("gx")
    place = jnp.stack(
        [lax.axis_index("gy") & 1, (row >> 2 & 1) * 8 + (row & 1) * 4 + (row >> 1 & 1) * 2]
    ).astype(jnp.int32)
    sent = pack(camera_of_device, point_feats, top_bin, front_bin, camera_embed)
    got = lax.all_to_all(sent, ("gx", "gy"), split_axis=0, concat_axis=0, tiled=True)
    mine, other, labels = pool_front(place, got)
    keep, send = pool_side(got, labels)
    mine = mine + swap(other, "gy", N_GY, 1)
    mine, keep, send = lax.optimization_barrier((mine, keep, send))
    top = pool_top(got, labels)
    shares = (front_share(mine), side_share(keep, send), top)
    front, side, top = lax.optimization_barrier(shares)
    mine = front_gather(front)
    mine, *sides = lax.optimization_barrier([mine] + side_gather(side))
    other = swap(mine, "gy", N_GY, 1)
    return mlp(place, top, mine, other, sides, w_in, b_in, w_out, b_out)


def solution(mesh):
    points = P(("gx", "gy"))
    placed = (P(("gx", "gy"), None), points, points, points, points, P(), P(), P(), P(), P())
    return jax.shard_map(
        per_device, mesh=mesh, in_specs=placed, out_specs=P("gx", "gy", None, None), check_vma=False
    )
```

```python
import jax
import jax.numpy as jnp
from jax import lax
from jax.experimental import pallas as pl
from jax.experimental.pallas import tpu as pltpu
from jax.sharding import PartitionSpec as P

C = 128
HID = 256
CAMS = 6
NZ = 32
BX = 64
BY = 16
P_DEV = 4096
DEVICES = 128
N_GX = 8
N_GY = 16
CAP = 64
ROWS = CAP + 8
SLOTS = DEVICES * CAP
CHUNKS = P_DEV // 128
PAIRS = DEVICES // 2

F32 = jnp.float32
BF16 = jnp.bfloat16
VMEM_LIMIT = 24 * 2**20
PACK_LIMIT = 60 * 2**20
MLP_LIMIT = 40 * 2**20


def iota(shape, axis):
    return lax.broadcasted_iota(jnp.int32, shape, axis)


def columns_of(rows):
    padding = jnp.zeros((128 - rows.shape[0], 128), F32)
    return jnp.concatenate([rows.astype(F32), padding], axis=0).T


def spread_column(columns, k):
    return jnp.broadcast_to(columns[:, k : k + 1], (128, 128)).astype(BF16)


def split_columns(values, half):
    zero = jnp.zeros_like(values)
    left = half == jnp.zeros_like(half)
    return jnp.concatenate([jnp.where(left, values, zero), jnp.where(left, zero, values)], axis=1)


def onehot_rows(label, base, rows):
    return jnp.where(iota((rows, 128), 0) + base == label, 1.0, 0.0).astype(BF16)


def onehot(labels_ref, base, rows, chunks):
    return jnp.concatenate(
        [onehot_rows(labels_ref[pl.ds(k, 1), :], base, rows) for k in range(chunks)], axis=1
    )


GROUPS = 4
GROUP = P_DEV // GROUPS
GROUP_CHUNKS = GROUP // 128


def pack_kernel(
    cam_ref, feats_hbm, top_hbm, front_hbm, embed_hbm, out_hbm,
    feats_ref, top_ref, front_ref, embed_ref, out_ref,
    marks_ref, rank_ref, place_ref, rhs_ref, values_ref, sorted_ref, stage_ref, meta_ref, start_ref, start_smem, sems,
):
    loads = [
        pltpu.make_async_copy(source, target, sems.at[i])
        for i, (source, target) in enumerate(
            [(top_hbm, top_ref), (front_hbm, front_ref), (embed_hbm, embed_ref), (feats_hbm, feats_ref)]
        )
    ]
    for load in loads:
        load.start()
    loads[0].wait()
    loads[1].wait()
    top = top_ref[...]
    live = top >= 0
    grid_x = top >> 8
    grid_y = top & 255
    owner = jnp.where(live, (grid_x >> 6) * N_GY + (grid_y >> 4), -1)
    cells = (
        (grid_x & (BX - 1)) + 1,
        (grid_y & (BY - 1)) + 1,
        (front_ref[...] & (NZ - 1)) + 1,
    )
    cells = [cell.astype(F32) for cell in cells]

    before = iota((128, 256), 0) < iota((128, 256), 1)
    later = iota((128, 256), 1) >= 128
    counter = jnp.where(before | later, 1.0, 0.0).astype(BF16)
    seen = jnp.zeros((DEVICES, 128), F32)
    slot = iota((CAP, 128), 0)
    bounds = [seen]
    for k in range(CHUNKS):
        columns = slice(k * 128, (k + 1) * 128)
        mine = iota((DEVICES, 128), 0) == owner[k : k + 1, :]
        marks = jnp.where(mine, 1.0, 0.0).astype(BF16)
        marks_ref[:, columns] = marks
        counts = jnp.dot(marks, counter, preferred_element_type=F32)
        rank = jnp.sum(jnp.where(mine, counts[:, :128] + seen, 0.0), axis=0, keepdims=True)
        seen = seen + counts[:, 128:]
        rank_ref[pl.ds(k, 1), :] = rank
        here = slot == rank.astype(jnp.int32)
        for part in range(3):
            values_ref[part * CAP : (part + 1) * CAP, columns] = jnp.where(
                here, cells[part][k : k + 1, :], 0.0
            ).astype(BF16)
        if (k + 1) % GROUP_CHUNKS == 0:
            bounds.append(seen)

    below = jnp.where(iota((128, 128), 1) < iota((128, 128), 0), 1.0, 0.0).astype(BF16)
    diagonal = iota((128, 128), 0) == iota((128, 128), 1)
    for g in range(GROUPS):
        count = bounds[g + 1] - bounds[g]
        starts = jnp.dot(below, count.astype(BF16), preferred_element_type=F32)
        for row, numbers in ((g, starts), (GROUPS + g, bounds[g])):
            line = jnp.sum(jnp.where(diagonal, numbers, 0.0), axis=0, keepdims=True)
            start_ref[pl.ds(row, 1), :] = line.astype(jnp.int32)
        shift = starts - bounds[g]
        for k in range(g * GROUP_CHUNKS, (g + 1) * GROUP_CHUNKS):
            mine = iota((DEVICES, 128), 0) == owner[k : k + 1, :]
            place_ref[pl.ds(k, 1), :] = rank_ref[pl.ds(k, 1), :] + jnp.sum(
                jnp.where(mine, shift, 0.0), axis=0, keepdims=True
            )
    copy = pltpu.make_async_copy(start_ref, start_smem, sems.at[4])
    copy.start()
    place = place_ref[...].astype(jnp.int32)
    halves = columns_of(place // (GROUP // 2))
    rank_ref[...] = jnp.where(live, place & (GROUP // 2 - 1), -1).astype(F32)

    loads[2].wait()
    loads[3].wait()
    camera = embed_ref[pl.ds(cam_ref[0], 1), :]
    for k in range(CHUNKS):
        rows = slice(k * 128, (k + 1) * 128)
        features = (feats_ref[rows, :].astype(F32) + camera).astype(BF16)
        rhs_ref[rows, :] = split_columns(features, spread_column(halves, k))

    for g in range(GROUPS):
        points = rhs_ref[g * GROUP : (g + 1) * GROUP, :]
        labels = [rank_ref[pl.ds(g * GROUP_CHUNKS + k, 1), :].astype(jnp.int32) for k in range(GROUP_CHUNKS)]
        for base in range(0, GROUP // 2, 256):
            picked = jnp.dot(
                jnp.concatenate([onehot_rows(label, base, 256) for label in labels], axis=1),
                points,
                preferred_element_type=F32,
            )
            sorted_ref[g, base : base + 256, :] = picked[:, :C]
            sorted_ref[g, GROUP // 2 + base : GROUP // 2 + base + 256, :] = picked[:, C:]
        sorted_ref[g, GROUP : GROUP + CAP, :] = jnp.zeros((CAP, C), F32)

    meta = lax.dot_general(
        values_ref[...], marks_ref[...], (((1,), (1,)), ((), ())), preferred_element_type=F32
    )
    for part in range(3):
        numbers = meta[part * CAP : (part + 1) * CAP, :]
        meta_ref[pl.ds(part, DEVICES, stride=8), :] = jnp.concatenate([numbers, numbers], axis=0).T
    for part in range(3, 8):
        meta_ref[pl.ds(part, DEVICES, stride=8), :] = jnp.zeros((DEVICES, 128), F32)
    out_ref[:, CAP:ROWS, :] = meta_ref[...].reshape(DEVICES, 8, 128).astype(BF16)

    copy.wait()
    stores = []
    for part in range(4):

        @pl.loop(0, DEVICES // 4, unroll=8)
        def _(i):
            device = part * (DEVICES // 4) + i
            base = device * CAP
            for g in range(GROUPS):
                run = sorted_ref[g, pl.ds(start_smem[g, device], CAP), :]
                stage_ref[pl.ds(base + start_smem[GROUPS + g, device], CAP), :] = run
            out_ref[device, 0:CAP, :] = stage_ref[pl.ds(base, CAP), :].astype(BF16)

        here = pl.ds(part * (DEVICES // 4), DEVICES // 4)
        stores.append(pltpu.make_async_copy(out_ref.at[here], out_hbm.at[here], sems.at[5 + part]))
        stores[-1].start()
    for store in stores:
        store.wait()


def pack(camera, point_feats, top_bin, front_bin, camera_embed):
    whole = pl.BlockSpec(memory_space=pltpu.HBM)
    return pl.pallas_call(
        pack_kernel,
        out_shape=jax.ShapeDtypeStruct((DEVICES, ROWS, C), BF16),
        in_specs=[pl.BlockSpec(memory_space=pltpu.SMEM)] + [whole] * 4,
        out_specs=whole,
        scratch_shapes=[
            pltpu.VMEM((P_DEV, C), BF16),
            pltpu.VMEM((CHUNKS, 128), jnp.int32),
            pltpu.VMEM((CHUNKS, 128), jnp.int32),
            pltpu.VMEM((CAMS, C), F32),
            pltpu.VMEM((DEVICES, ROWS, C), BF16),
            pltpu.VMEM((DEVICES, P_DEV), BF16),
            pltpu.VMEM((CHUNKS, 128), F32),
            pltpu.VMEM((CHUNKS, 128), F32),
            pltpu.VMEM((P_DEV, 2 * C), BF16),
            pltpu.VMEM((3 * CAP, P_DEV), BF16),
            pltpu.VMEM((GROUPS, GROUP + CAP, C), F32),
            pltpu.VMEM((SLOTS + CAP, C), F32),
            pltpu.VMEM((DEVICES * 8, 128), F32),
            pltpu.VMEM((2 * GROUPS, DEVICES), jnp.int32),
            pltpu.SMEM((2 * GROUPS, DEVICES), jnp.int32),
            pltpu.SemaphoreType.DMA((9,)),
        ],
        compiler_params=pltpu.CompilerParams(vmem_limit_bytes=PACK_LIMIT),
        cost_estimate=pl.CostEstimate(flops=2 * 4096 * 4096 * 256, bytes_accessed=4 * 2**20, transcendentals=0),
        name="pack",
    )(camera, point_feats, top_bin.reshape(CHUNKS, 128), front_bin.reshape(CHUNKS, 128), camera_embed)


def split_points(got_ref, half_ref, rhs_ref):
    halves = columns_of(half_ref[...])
    for q in range(PAIRS):
        piece = got_ref[q * 2 : q * 2 + 2, 0:CAP, :].reshape(128, C)
        rhs_ref[q * 128 : (q + 1) * 128, :] = split_columns(piece, spread_column(halves, q))


def pool_front_kernel(place_ref, got_ref, mine_ref, other_ref, labels_ref, rhs_ref, meta_ref):
    meta_ref[...] = got_ref[:, CAP:ROWS, :].astype(F32).reshape(DEVICES * 8, 128)
    first = iota((PAIRS, 128), 1) < CAP

    def pairs(part):
        even = meta_ref[pl.ds(part, PAIRS, stride=16), :]
        odd = meta_ref[pl.ds(part + 8, PAIRS, stride=16), :]
        return jnp.where(first, even, odd).astype(jnp.int32) - 1

    x, y, z = pairs(0), pairs(1), pairs(2)
    live = x >= 0
    x = x ^ (place_ref[0] * (BX // 2))
    labels_ref[0] = jnp.where(live, x * 16 + (z & 15), -1)
    labels_ref[1] = jnp.where(live, x * 8 + (y & 7), -1)
    labels_ref[2] = jnp.where(live, (y ^ place_ref[1]) * 16 + (z & 15), -1)
    labels_ref[3] = (y >> 3) & 1
    labels_ref[4] = (z >> 4) & 1
    split_points(got_ref, labels_ref.at[4], rhs_ref)
    for block in range(4):
        sums = jnp.dot(onehot(labels_ref.at[0], block * 256, 256, PAIRS), rhs_ref[...], preferred_element_type=F32)
        out = (mine_ref, other_ref)[block // 2]
        xs = pl.ds(block % 2 * 16, 16)
        out[xs, 0:16, :] = sums[:, :C].reshape(16, 16, C)
        out[xs, 16:32, :] = sums[:, C:].reshape(16, 16, C)


def pool_side_kernel(rhs_ref, labels_ref, keep_ref, send_ref):
    sums = jnp.dot(onehot(labels_ref.at[2], 0, 256, PAIRS), rhs_ref[...], preferred_element_type=F32)
    for half, out in enumerate((keep_ref, send_ref)):
        rows = slice(half * 128, (half + 1) * 128)
        out[:, 0:16, :] = sums[rows, :C].reshape(BY // 2, 16, C)
        out[:, 16:32, :] = sums[rows, C:].reshape(BY // 2, 16, C)


def pool_top_kernel(got_ref, labels_ref, top_ref, rhs_ref):
    split_points(got_ref, labels_ref.at[3], rhs_ref)
    for block in range(2):
        sums = jnp.dot(onehot(labels_ref.at[1], block * 256, 256, PAIRS), rhs_ref[...], preferred_element_type=F32)
        halves = [sums[:, :C].reshape(32, 8, C), sums[:, C:].reshape(32, 8, C)]
        top_ref[pl.ds(block * 32, 32)] = jnp.concatenate(halves, axis=1).astype(BF16)


def call(kernel, ins, outs, scratch, flops, name):
    whole = pl.BlockSpec(memory_space=pltpu.VMEM)
    small = pl.BlockSpec(memory_space=pltpu.SMEM)
    return pl.pallas_call(
        kernel,
        out_shape=outs,
        in_specs=[small if i.dtype == jnp.int32 and i.size == 2 else whole for i in ins],
        out_specs=[whole] * len(outs),
        scratch_shapes=scratch,
        compiler_params=pltpu.CompilerParams(vmem_limit_bytes=VMEM_LIMIT),
        cost_estimate=pl.CostEstimate(flops=flops, bytes_accessed=flops // 1024, transcendentals=0),
        name=name,
    )(*ins)


def pool_front(place, got):
    shape = jax.ShapeDtypeStruct((BX // 2, NZ, C), F32)
    labels = jax.ShapeDtypeStruct((5, PAIRS, 128), jnp.int32)
    points = jax.ShapeDtypeStruct((SLOTS, 2 * C), BF16)
    scratch = [pltpu.VMEM((DEVICES * 8, 128), F32)]
    flops = 2 * 8192 * 1024 * 256 * 2
    return call(pool_front_kernel, [place, got], [shape, shape, labels, points], scratch, flops, "pool_front")


def pool_side(points, labels):
    shape = jax.ShapeDtypeStruct((BY // 2, NZ, C), F32)
    return call(pool_side_kernel, [points, labels], [shape, shape], [], 2 * 8192 * 512 * 256, "pool_side")


def fold_kernel(keep_ref, got_ref, *out_refs):
    for k, out in enumerate(out_refs):
        rows = pl.ds(k * 2, 2)
        out[...] = keep_ref[rows] + got_ref[rows]


def fold(keep, got):
    shape = jax.ShapeDtypeStruct((2, NZ, C), F32)
    return call(fold_kernel, [keep, got], [shape] * 4, [], 1024, "fold")


def pool_top(got, labels):
    return call(
        pool_top_kernel,
        [got, labels],
        [jax.ShapeDtypeStruct((BX, BY, C), BF16)],
        [pltpu.VMEM((SLOTS, 2 * C), BF16)],
        1024,
        "pool_top",
    )[0]


STEP = 16
HALF_STEPS = BX // STEP // 2


def mlp_kernel(
    place_ref, top_ref, mine_ref, other_ref, s0_ref, s1_ref, s2_ref, s3_ref,
    w_in_ref, b_in_ref, w_out_ref, b_out_ref, out_ref, side_ref, wide_ref, half_ref,
):
    @pl.when(pl.program_id(0) == 0)
    def _():
        for k, rows in enumerate((s0_ref, s1_ref, s2_ref, s3_ref)):
            for j in range(4):
                y = k * 2 + j if j < 2 else BY // 2 + k * 2 + j - 2
                side_ref[y ^ place_ref[1]] = rows[j].astype(F32)
        bias = b_in_ref[...]
        high = bias.astype(BF16).astype(F32)
        middle = (bias - high).astype(BF16).astype(F32)
        low = bias - high - middle
        row = iota((C, HID), 0)
        rest = jnp.where(row == 0, high, jnp.where(row == 1, middle, jnp.where(row == 2, low, 0.0)))
        wide_ref[0:C, :] = w_in_ref[...]
        wide_ref[C : 2 * C, :] = rest.astype(BF16)
        half_ref[...] = (w_out_ref[...].astype(F32) * 0.5).astype(BF16)

    mine = pl.program_id(0) < HALF_STEPS
    ones = jnp.where(iota((BY * NZ, C), 1) < 3, 1.0, 0.0).astype(BF16)
    for i in range(STEP):
        top = top_ref[i].astype(F32)
        front = jnp.where(mine, mine_ref[i].astype(F32), other_ref[i].astype(F32))
        cell = (top[:, None, :] + front[None, :, :] + side_ref[...]).astype(BF16).reshape(BY * NZ, C)
        inner = jnp.dot(jnp.concatenate([cell, ones], axis=1), wide_ref[...], preferred_element_type=F32)
        twice = (inner * (1.0 + lax.erf(inner * 0.7071067811865476))).astype(BF16)
        result = jnp.dot(twice, half_ref[...], preferred_element_type=F32)
        result = result + (b_out_ref[...] + cell.astype(F32))
        out_ref[i] = result.astype(BF16).reshape(BY, NZ, C)


def mlp(place, top, mine, other, sides, w_in, b_in, w_out, b_out):
    def same(*shape):
        return pl.BlockSpec(shape, lambda i, h: (0,) * len(shape))

    return pl.pallas_call(
        mlp_kernel,
        grid_spec=pltpu.PrefetchScalarGridSpec(
            num_scalar_prefetch=1,
            grid=(BX // STEP,),
            in_specs=[
                pl.BlockSpec((STEP, BY, C), lambda i, h: (i, 0, 0)),
                pl.BlockSpec((STEP, NZ, C), lambda i, h: (jnp.minimum(i, HALF_STEPS - 1), 0, 0)),
                pl.BlockSpec((STEP, NZ, C), lambda i, h: (jnp.maximum(i - HALF_STEPS, 0), 0, 0)),
            ]
            + [same(4, NZ, C)] * 4
            + [same(C, HID), same(1, HID), same(HID, C), same(1, C)],
            out_specs=pl.BlockSpec((STEP, BY, NZ, C), lambda i, h: (i ^ (h[0] * HALF_STEPS), 0, 0, 0)),
            scratch_shapes=[
                pltpu.VMEM((BY, NZ, C), F32),
                pltpu.VMEM((2 * C, HID), BF16),
                pltpu.VMEM((HID, C), BF16),
            ],
        ),
        out_shape=jax.ShapeDtypeStruct((BX, BY, NZ, C), BF16),
        compiler_params=pltpu.CompilerParams(vmem_limit_bytes=MLP_LIMIT),
        cost_estimate=pl.CostEstimate(
            flops=4 * BX * BY * NZ * C * HID, bytes_accessed=9 * 2**20, transcendentals=BX * BY * NZ * HID
        ),
        name="voxel_mlp",
    )(place, top, mine, other, *sides, w_in, b_in.reshape(1, HID), w_out, b_out.reshape(1, C))


SAME_CORE = [list(range(core, N_GY, 2)) for core in range(2)]


def swap(array, axis, size, bit):
    return lax.ppermute(array, axis, [(i, i ^ bit) for i in range(size)])


def spread_kernel(pieces_ref, out_ref):
    share = jnp.sum(pieces_ref[...], axis=0).astype(BF16)
    for i in range(8):
        out_ref[i] = share


def front_share(mine):
    pieces = mine.reshape(8, mine.shape[0] * mine.shape[1] // 8, C)
    pieces = lax.all_to_all(pieces, "gy", 0, 0, tiled=True, axis_index_groups=SAME_CORE)
    return call(spread_kernel, [pieces], [jax.ShapeDtypeStruct(pieces.shape, BF16)], [], 1024, "spread")[0]


def front_gather(copies):
    whole = lax.all_to_all(copies, "gy", 0, 0, tiled=True, axis_index_groups=SAME_CORE)
    return whole.reshape(BX // 2, NZ, C)


def side_share(keep, send):
    parts = fold(keep, swap(send, "gx", N_GX, 4))
    share = (
        parts[0] + swap(parts[1], "gx", N_GX, 2) + swap(parts[2], "gx", N_GX, 1) + swap(parts[3], "gx", N_GX, 3)
    ).astype(BF16)
    return jnp.concatenate([share, swap(share, "gx", N_GX, 4)], axis=0)


def side_gather(share):
    return [share] + [swap(share, "gx", N_GX, bit) for bit in (2, 1, 3)]


def per_device(
    point_feats, top_bin, front_bin, side_bin, camera_of_device, camera_embed, w_in, b_in, w_out, b_out
):
    row = lax.axis_index("gx")
    place = jnp.stack(
        [lax.axis_index("gy") & 1, (row >> 2 & 1) * 8 + (row & 1) * 4 + (row >> 1 & 1) * 2]
    ).astype(jnp.int32)
    sent = pack(camera_of_device, point_feats, top_bin, front_bin, camera_embed)
    got = lax.all_to_all(sent, ("gx", "gy"), split_axis=0, concat_axis=0, tiled=True)
    mine, other, labels, points = pool_front(place, got)
    keep, send = pool_side(points, labels)
    mine = mine + swap(other, "gy", N_GY, 1)
    mine, keep, send = lax.optimization_barrier((mine, keep, send))
    top = pool_top(got, labels)
    front, side = lax.optimization_barrier((front_share(mine), side_share(keep, send)))
    mine = front_gather(front)
    mine, top, *sides = lax.optimization_barrier([mine, top] + side_gather(side))
    other = swap(mine, "gy", N_GY, 1)
    return mlp(place, top, mine, other, sides, w_in, b_in, w_out, b_out)


def solution(mesh):
    points = P(("gx", "gy"))
    placed = (P(("gx", "gy"), None), points, points, points, points, P(), P(), P(), P(), P())
    return jax.shard_map(
        per_device, mesh=mesh, in_specs=placed, out_specs=P("gx", "gy", None, None), check_vma=False
    )
```

```python
import jax
import jax.numpy as jnp
from jax import lax
from jax.experimental import pallas as pl
from jax.experimental.pallas import tpu as pltpu
from jax.sharding import PartitionSpec as P

C = 128
HID = 256
CAMS = 6
NZ = 32
BX = 64
BY = 16
P_DEV = 4096
DEVICES = 128
N_GX = 8
N_GY = 16
CAP = 64
ROWS = CAP + 8
SLOTS = DEVICES * CAP
CHUNKS = P_DEV // 128
PAIRS = DEVICES // 2

F32 = jnp.float32
BF16 = jnp.bfloat16
VMEM_LIMIT = 24 * 2**20
PACK_LIMIT = 60 * 2**20
MLP_LIMIT = 40 * 2**20


def iota(shape, axis):
    return lax.broadcasted_iota(jnp.int32, shape, axis)


def columns_of(rows):
    padding = jnp.zeros((128 - rows.shape[0], 128), F32)
    return jnp.concatenate([rows.astype(F32), padding], axis=0).T


def spread_column(columns, k):
    return jnp.broadcast_to(columns[:, k : k + 1], (128, 128)).astype(BF16)


def split_columns(values, half):
    zero = jnp.zeros_like(values)
    left = half == jnp.zeros_like(half)
    return jnp.concatenate([jnp.where(left, values, zero), jnp.where(left, zero, values)], axis=1)


def onehot_rows(label, base, rows):
    return jnp.where(iota((rows, 128), 0) + base == label, 1.0, 0.0).astype(BF16)


def onehot(labels_ref, base, rows, chunks):
    return jnp.concatenate(
        [onehot_rows(labels_ref[pl.ds(k, 1), :], base, rows) for k in range(chunks)], axis=1
    )


GROUPS = 4
GROUP = P_DEV // GROUPS
GROUP_CHUNKS = GROUP // 128


def pack_kernel(
    cam_ref, feats_hbm, top_hbm, front_hbm, embed_hbm, out_hbm,
    feats_ref, top_ref, front_ref, embed_ref, out_ref,
    marks_ref, rank_ref, place_ref, rhs_ref, values_ref, sorted_ref, stage_ref, meta_ref, start_ref, start_smem, sems,
):
    loads = [
        pltpu.make_async_copy(source, target, sems.at[i])
        for i, (source, target) in enumerate(
            [(top_hbm, top_ref), (front_hbm, front_ref), (embed_hbm, embed_ref), (feats_hbm, feats_ref)]
        )
    ]
    for load in loads:
        load.start()
    loads[0].wait()
    loads[1].wait()
    top = top_ref[...]
    live = top >= 0
    grid_x = top >> 8
    grid_y = top & 255
    owner = jnp.where(live, (grid_x >> 6) * N_GY + (grid_y >> 4), -1)
    cells = (
        (grid_x & (BX - 1)) + 1,
        (grid_y & (BY - 1)) + 1,
        (front_ref[...] & (NZ - 1)) + 1,
    )
    cells = [cell.astype(F32) for cell in cells]

    before = iota((128, 256), 0) < iota((128, 256), 1)
    later = iota((128, 256), 1) >= 128
    counter = jnp.where(before | later, 1.0, 0.0).astype(BF16)
    seen = jnp.zeros((DEVICES, 128), F32)
    slot = iota((CAP, 128), 0)
    bounds = [seen]
    for k in range(CHUNKS):
        columns = slice(k * 128, (k + 1) * 128)
        mine = iota((DEVICES, 128), 0) == owner[k : k + 1, :]
        marks = jnp.where(mine, 1.0, 0.0).astype(BF16)
        marks_ref[:, columns] = marks
        counts = jnp.dot(marks, counter, preferred_element_type=F32)
        rank = jnp.sum(jnp.where(mine, counts[:, :128] + seen, 0.0), axis=0, keepdims=True)
        seen = seen + counts[:, 128:]
        rank_ref[pl.ds(k, 1), :] = rank
        here = slot == rank.astype(jnp.int32)
        for part in range(3):
            values_ref[part * CAP : (part + 1) * CAP, columns] = jnp.where(
                here, cells[part][k : k + 1, :], 0.0
            ).astype(BF16)
        if (k + 1) % GROUP_CHUNKS == 0:
            bounds.append(seen)

    below = jnp.where(iota((128, 128), 1) < iota((128, 128), 0), 1.0, 0.0).astype(BF16)
    diagonal = iota((128, 128), 0) == iota((128, 128), 1)
    for g in range(GROUPS):
        count = bounds[g + 1] - bounds[g]
        starts = jnp.dot(below, count.astype(BF16), preferred_element_type=F32)
        for row, numbers in ((g, starts), (GROUPS + g, bounds[g])):
            line = jnp.sum(jnp.where(diagonal, numbers, 0.0), axis=0, keepdims=True)
            start_ref[pl.ds(row, 1), :] = line.astype(jnp.int32)
        shift = starts - bounds[g]
        for k in range(g * GROUP_CHUNKS, (g + 1) * GROUP_CHUNKS):
            mine = iota((DEVICES, 128), 0) == owner[k : k + 1, :]
            place_ref[pl.ds(k, 1), :] = rank_ref[pl.ds(k, 1), :] + jnp.sum(
                jnp.where(mine, shift, 0.0), axis=0, keepdims=True
            )
    copy = pltpu.make_async_copy(start_ref, start_smem, sems.at[4])
    copy.start()
    place = place_ref[...].astype(jnp.int32)
    halves = columns_of(place // (GROUP // 2))
    rank_ref[...] = jnp.where(live, place & (GROUP // 2 - 1), -1).astype(F32)

    loads[2].wait()
    loads[3].wait()
    camera = embed_ref[pl.ds(cam_ref[0], 1), :]
    for k in range(CHUNKS):
        rows = slice(k * 128, (k + 1) * 128)
        features = (feats_ref[rows, :].astype(F32) + camera).astype(BF16)
        rhs_ref[rows, :] = split_columns(features, spread_column(halves, k))

    for g in range(GROUPS):
        points = rhs_ref[g * GROUP : (g + 1) * GROUP, :]
        labels = [rank_ref[pl.ds(g * GROUP_CHUNKS + k, 1), :].astype(jnp.int32) for k in range(GROUP_CHUNKS)]
        for base in range(0, GROUP // 2, 256):
            picked = jnp.dot(
                jnp.concatenate([onehot_rows(label, base, 256) for label in labels], axis=1),
                points,
                preferred_element_type=F32,
            )
            sorted_ref[g, base : base + 256, :] = picked[:, :C]
            sorted_ref[g, GROUP // 2 + base : GROUP // 2 + base + 256, :] = picked[:, C:]
        sorted_ref[g, GROUP : GROUP + CAP, :] = jnp.zeros((CAP, C), F32)

    meta = lax.dot_general(
        values_ref[...], marks_ref[...], (((1,), (1,)), ((), ())), preferred_element_type=F32
    )
    for part in range(3):
        numbers = meta[part * CAP : (part + 1) * CAP, :]
        meta_ref[pl.ds(part, DEVICES, stride=8), :] = jnp.concatenate([numbers, numbers], axis=0).T
    for part in range(3, 8):
        meta_ref[pl.ds(part, DEVICES, stride=8), :] = jnp.zeros((DEVICES, 128), F32)
    out_ref[:, CAP:ROWS, :] = meta_ref[...].reshape(DEVICES, 8, 128).astype(BF16)

    copy.wait()
    stores = []
    for part in range(4):

        @pl.loop(0, DEVICES // 4, unroll=8)
        def _(i):
            device = part * (DEVICES // 4) + i
            base = device * CAP
            for g in range(GROUPS):
                run = sorted_ref[g, pl.ds(start_smem[g, device], CAP), :]
                stage_ref[pl.ds(base + start_smem[GROUPS + g, device], CAP), :] = run
            out_ref[device, 0:CAP, :] = stage_ref[pl.ds(base, CAP), :].astype(BF16)

        here = pl.ds(part * (DEVICES // 4), DEVICES // 4)
        stores.append(pltpu.make_async_copy(out_ref.at[here], out_hbm.at[here], sems.at[5 + part]))
        stores[-1].start()
    for store in stores:
        store.wait()


def pack(camera, point_feats, top_bin, front_bin, camera_embed):
    whole = pl.BlockSpec(memory_space=pltpu.HBM)
    return pl.pallas_call(
        pack_kernel,
        out_shape=jax.ShapeDtypeStruct((DEVICES, ROWS, C), BF16),
        in_specs=[pl.BlockSpec(memory_space=pltpu.SMEM)] + [whole] * 4,
        out_specs=whole,
        scratch_shapes=[
            pltpu.VMEM((P_DEV, C), BF16),
            pltpu.VMEM((CHUNKS, 128), jnp.int32),
            pltpu.VMEM((CHUNKS, 128), jnp.int32),
            pltpu.VMEM((CAMS, C), F32),
            pltpu.VMEM((DEVICES, ROWS, C), BF16),
            pltpu.VMEM((DEVICES, P_DEV), BF16),
            pltpu.VMEM((CHUNKS, 128), F32),
            pltpu.VMEM((CHUNKS, 128), F32),
            pltpu.VMEM((P_DEV, 2 * C), BF16),
            pltpu.VMEM((3 * CAP, P_DEV), BF16),
            pltpu.VMEM((GROUPS, GROUP + CAP, C), F32),
            pltpu.VMEM((SLOTS + CAP, C), F32),
            pltpu.VMEM((DEVICES * 8, 128), F32),
            pltpu.VMEM((2 * GROUPS, DEVICES), jnp.int32),
            pltpu.SMEM((2 * GROUPS, DEVICES), jnp.int32),
            pltpu.SemaphoreType.DMA((9,)),
        ],
        compiler_params=pltpu.CompilerParams(vmem_limit_bytes=PACK_LIMIT),
        cost_estimate=pl.CostEstimate(flops=2 * 4096 * 4096 * 256, bytes_accessed=4 * 2**20, transcendentals=0),
        name="pack",
    )(camera, point_feats, top_bin.reshape(CHUNKS, 128), front_bin.reshape(CHUNKS, 128), camera_embed)


def split_points(got_ref, half_ref, rhs_ref):
    halves = columns_of(half_ref[...])
    for q in range(PAIRS):
        piece = got_ref[q * 2 : q * 2 + 2, 0:CAP, :].reshape(128, C)
        rhs_ref[q * 128 : (q + 1) * 128, :] = split_columns(piece, spread_column(halves, q))


def pool_front_kernel(place_ref, got_ref, mine_ref, other_ref, labels_ref, rhs_ref, meta_ref):
    meta_ref[...] = got_ref[:, CAP:ROWS, :].astype(F32).reshape(DEVICES * 8, 128)
    first = iota((PAIRS, 128), 1) < CAP

    def pairs(part):
        even = meta_ref[pl.ds(part, PAIRS, stride=16), :]
        odd = meta_ref[pl.ds(part + 8, PAIRS, stride=16), :]
        return jnp.where(first, even, odd).astype(jnp.int32) - 1

    x, y, z = pairs(0), pairs(1), pairs(2)
    live = x >= 0
    x = x ^ (place_ref[0] * (BX // 2))
    labels_ref[0] = jnp.where(live, x * 16 + (z & 15), -1)
    labels_ref[1] = jnp.where(live, x * 8 + (y & 7), -1)
    labels_ref[2] = jnp.where(live, (y ^ place_ref[1]) * 16 + (z & 15), -1)
    labels_ref[3] = (y >> 3) & 1
    labels_ref[4] = (z >> 4) & 1
    split_points(got_ref, labels_ref.at[4], rhs_ref)
    for block in range(4):
        sums = jnp.dot(onehot(labels_ref.at[0], block * 256, 256, PAIRS), rhs_ref[...], preferred_element_type=F32)
        out = (mine_ref, other_ref)[block // 2]
        xs = pl.ds(block % 2 * 16, 16)
        out[xs, 0:16, :] = sums[:, :C].reshape(16, 16, C)
        out[xs, 16:32, :] = sums[:, C:].reshape(16, 16, C)


def pool_side_kernel(rhs_ref, labels_ref, keep_ref, send_ref):
    sums = jnp.dot(onehot(labels_ref.at[2], 0, 256, PAIRS), rhs_ref[...], preferred_element_type=F32)
    for half, out in enumerate((keep_ref, send_ref)):
        rows = slice(half * 128, (half + 1) * 128)
        out[:, 0:16, :] = sums[rows, :C].reshape(BY // 2, 16, C)
        out[:, 16:32, :] = sums[rows, C:].reshape(BY // 2, 16, C)


def pool_top_kernel(got_ref, labels_ref, top_ref, rhs_ref):
    split_points(got_ref, labels_ref.at[3], rhs_ref)
    for block in range(2):
        sums = jnp.dot(onehot(labels_ref.at[1], block * 256, 256, PAIRS), rhs_ref[...], preferred_element_type=F32)
        halves = [sums[:, :C].reshape(32, 8, C), sums[:, C:].reshape(32, 8, C)]
        top_ref[pl.ds(block * 32, 32)] = jnp.concatenate(halves, axis=1).astype(BF16)


def call(kernel, ins, outs, scratch, flops, name):
    whole = pl.BlockSpec(memory_space=pltpu.VMEM)
    small = pl.BlockSpec(memory_space=pltpu.SMEM)
    return pl.pallas_call(
        kernel,
        out_shape=outs,
        in_specs=[small if i.dtype == jnp.int32 and i.size == 2 else whole for i in ins],
        out_specs=[whole] * len(outs),
        scratch_shapes=scratch,
        compiler_params=pltpu.CompilerParams(vmem_limit_bytes=VMEM_LIMIT),
        cost_estimate=pl.CostEstimate(flops=flops, bytes_accessed=flops // 1024, transcendentals=0),
        name=name,
    )(*ins)


def pool_front(place, got):
    shape = jax.ShapeDtypeStruct((BX // 2, NZ, C), F32)
    labels = jax.ShapeDtypeStruct((5, PAIRS, 128), jnp.int32)
    points = jax.ShapeDtypeStruct((SLOTS, 2 * C), BF16)
    scratch = [pltpu.VMEM((DEVICES * 8, 128), F32)]
    flops = 2 * 8192 * 1024 * 256 * 2
    return call(pool_front_kernel, [place, got], [shape, shape, labels, points], scratch, flops, "pool_front")


def pool_side(points, labels):
    shape = jax.ShapeDtypeStruct((BY // 2, NZ, C), F32)
    return call(pool_side_kernel, [points, labels], [shape, shape], [], 2 * 8192 * 512 * 256, "pool_side")


def pool_top(got, labels):
    return call(
        pool_top_kernel,
        [got, labels],
        [jax.ShapeDtypeStruct((BX, BY, C), BF16)],
        [pltpu.VMEM((SLOTS, 2 * C), BF16)],
        1024,
        "pool_top",
    )[0]


STEP = 16
HALF_STEPS = BX // STEP // 2


def mlp_kernel(
    place_ref, top_ref, mine_ref, other_ref, near_ref, far_ref,
    w_in_ref, b_in_ref, w_out_ref, b_out_ref, out_ref, side_ref, wide_ref, half_ref,
):
    @pl.when(pl.program_id(0) == 0)
    def _():
        for y in range(BY // 2):
            side_ref[y ^ place_ref[1]] = near_ref[y].astype(F32)
            side_ref[(y + BY // 2) ^ place_ref[1]] = far_ref[y].astype(F32)
        bias = b_in_ref[...]
        high = bias.astype(BF16).astype(F32)
        middle = (bias - high).astype(BF16).astype(F32)
        low = bias - high - middle
        row = iota((C, HID), 0)
        rest = jnp.where(row == 0, high, jnp.where(row == 1, middle, jnp.where(row == 2, low, 0.0)))
        wide_ref[0:C, :] = w_in_ref[...]
        wide_ref[C : 2 * C, :] = rest.astype(BF16)
        half_ref[...] = (w_out_ref[...].astype(F32) * 0.5).astype(BF16)

    mine = pl.program_id(0) < HALF_STEPS
    ones = jnp.where(iota((BY * NZ, C), 1) < 3, 1.0, 0.0).astype(BF16)
    for i in range(STEP):
        top = top_ref[i].astype(F32)
        front = jnp.where(mine, mine_ref[i].astype(F32), other_ref[i].astype(F32))
        cell = (top[:, None, :] + front[None, :, :] + side_ref[...]).astype(BF16).reshape(BY * NZ, C)
        inner = jnp.dot(jnp.concatenate([cell, ones], axis=1), wide_ref[...], preferred_element_type=F32)
        twice = (inner * (1.0 + lax.erf(inner * 0.7071067811865476))).astype(BF16)
        result = jnp.dot(twice, half_ref[...], preferred_element_type=F32)
        result = result + (b_out_ref[...] + cell.astype(F32))
        out_ref[i] = result.astype(BF16).reshape(BY, NZ, C)


def mlp(place, top, mine, other, near, far, w_in, b_in, w_out, b_out):
    def same(*shape):
        return pl.BlockSpec(shape, lambda i, h: (0,) * len(shape))

    return pl.pallas_call(
        mlp_kernel,
        grid_spec=pltpu.PrefetchScalarGridSpec(
            num_scalar_prefetch=1,
            grid=(BX // STEP,),
            in_specs=[
                pl.BlockSpec((STEP, BY, C), lambda i, h: (i, 0, 0)),
                pl.BlockSpec((STEP, NZ, C), lambda i, h: (jnp.minimum(i, HALF_STEPS - 1), 0, 0)),
                pl.BlockSpec((STEP, NZ, C), lambda i, h: (jnp.maximum(i - HALF_STEPS, 0), 0, 0)),
            ]
            + [same(BY // 2, NZ, C)] * 2
            + [same(C, HID), same(1, HID), same(HID, C), same(1, C)],
            out_specs=pl.BlockSpec((STEP, BY, NZ, C), lambda i, h: (i ^ (h[0] * HALF_STEPS), 0, 0, 0)),
            scratch_shapes=[
                pltpu.VMEM((BY, NZ, C), F32),
                pltpu.VMEM((2 * C, HID), BF16),
                pltpu.VMEM((HID, C), BF16),
            ],
        ),
        out_shape=jax.ShapeDtypeStruct((BX, BY, NZ, C), BF16),
        compiler_params=pltpu.CompilerParams(vmem_limit_bytes=MLP_LIMIT),
        cost_estimate=pl.CostEstimate(
            flops=4 * BX * BY * NZ * C * HID, bytes_accessed=9 * 2**20, transcendentals=BX * BY * NZ * HID
        ),
        name="voxel_mlp",
    )(place, top, mine, other, near, far, w_in, b_in.reshape(1, HID), w_out, b_out.reshape(1, C))


SAME_CORE = [list(range(core, N_GY, 2)) for core in range(2)]


def swap(array, axis, size, bit):
    return lax.ppermute(array, axis, [(i, i ^ bit) for i in range(size)])


def spread_kernel(pieces_ref, out_ref):
    share = jnp.sum(pieces_ref[...], axis=0).astype(BF16)
    for i in range(8):
        out_ref[i] = share


def front_share(mine):
    pieces = mine.reshape(8, mine.shape[0] * mine.shape[1] // 8, C)
    pieces = lax.all_to_all(pieces, "gy", 0, 0, tiled=True, axis_index_groups=SAME_CORE)
    return call(spread_kernel, [pieces], [jax.ShapeDtypeStruct(pieces.shape, BF16)], [], 1024, "spread")[0]


def front_gather(copies):
    whole = lax.all_to_all(copies, "gy", 0, 0, tiled=True, axis_index_groups=SAME_CORE)
    return whole.reshape(BX // 2, NZ, C)


def sum_kernel(mine_ref, got_ref, out_ref):
    out_ref[...] = mine_ref[...] + got_ref[...]


def pair_sum(mine, got):
    return call(sum_kernel, [mine, got], [jax.ShapeDtypeStruct(mine.shape, F32)], [], 1024, "pair_sum")[0]


def side_near(keep, send):
    part = pair_sum(keep, swap(send, "gx", N_GX, 4))
    others = [swap(part, "gx", N_GX, bit) for bit in (2, 1, 3)]
    return (part + others[0] + others[1] + others[2]).astype(BF16)


def per_device(
    point_feats, top_bin, front_bin, side_bin, camera_of_device, camera_embed, w_in, b_in, w_out, b_out
):
    row = lax.axis_index("gx")
    place = jnp.stack(
        [lax.axis_index("gy") & 1, (row >> 2 & 1) * (BY // 2)]
    ).astype(jnp.int32)
    sent = pack(camera_of_device, point_feats, top_bin, front_bin, camera_embed)
    got = lax.all_to_all(sent, ("gx", "gy"), split_axis=0, concat_axis=0, tiled=True)
    mine, other, labels, points = pool_front(place, got)
    keep, send = pool_side(points, labels)
    mine = pair_sum(mine, swap(other, "gy", N_GY, 1))
    mine, keep, send = lax.optimization_barrier((mine, keep, send))
    top = pool_top(got, labels)
    front, near = lax.optimization_barrier((front_share(mine), side_near(keep, send)))
    mine = front_gather(front)
    mine, top, near, far = lax.optimization_barrier((mine, top, near, swap(near, "gx", N_GX, 4)))
    other = swap(mine, "gy", N_GY, 1)
    return mlp(place, top, mine, other, near, far, w_in, b_in, w_out, b_out)


def solution(mesh):
    points = P(("gx", "gy"))
    placed = (P(("gx", "gy"), None), points, points, points, points, P(), P(), P(), P(), P())
    return jax.shard_map(
        per_device, mesh=mesh, in_specs=placed, out_specs=P("gx", "gy", None, None), check_vma=False
    )
```

```python
import jax
import jax.numpy as jnp
from jax import lax
from jax.experimental import pallas as pl
from jax.experimental.pallas import tpu as pltpu
from jax.sharding import PartitionSpec as P

C = 128
HID = 256
CAMS = 6
NZ = 32
BX = 64
BY = 16
P_DEV = 4096
DEVICES = 128
N_GX = 8
N_GY = 16
CAP = 64
ROWS = CAP + 8
SLOTS = DEVICES * CAP
CHUNKS = P_DEV // 128
PAIRS = DEVICES // 2

F32 = jnp.float32
BF16 = jnp.bfloat16
VMEM_LIMIT = 24 * 2**20
PACK_LIMIT = 60 * 2**20
MLP_LIMIT = 40 * 2**20


def iota(shape, axis):
    return lax.broadcasted_iota(jnp.int32, shape, axis)


def columns_of(rows):
    padding = jnp.zeros((128 - rows.shape[0], 128), F32)
    return jnp.concatenate([rows.astype(F32), padding], axis=0).T


def spread_column(columns, k):
    return jnp.broadcast_to(columns[:, k : k + 1], (128, 128)).astype(BF16)


def split_columns(values, half):
    zero = jnp.zeros_like(values)
    left = half == jnp.zeros_like(half)
    return jnp.concatenate([jnp.where(left, values, zero), jnp.where(left, zero, values)], axis=1)


def onehot_rows(label, base, rows):
    return jnp.where(iota((rows, 128), 0) + base == label, 1.0, 0.0).astype(BF16)


def onehot(labels_ref, base, rows, chunks):
    return jnp.concatenate(
        [onehot_rows(labels_ref[pl.ds(k, 1), :], base, rows) for k in range(chunks)], axis=1
    )


GROUPS = 4
GROUP = P_DEV // GROUPS
GROUP_CHUNKS = GROUP // 128


def pack_kernel(
    cam_ref, feats_hbm, top_hbm, front_hbm, embed_hbm, out_hbm,
    feats_ref, top_ref, front_ref, embed_ref, out_ref,
    marks_ref, rank_ref, place_ref, rhs_ref, values_ref, sorted_ref, stage_ref, meta_ref, start_ref, start_smem, sems,
):
    loads = [
        pltpu.make_async_copy(source, target, sems.at[i])
        for i, (source, target) in enumerate(
            [(top_hbm, top_ref), (front_hbm, front_ref), (embed_hbm, embed_ref), (feats_hbm, feats_ref)]
        )
    ]
    for load in loads:
        load.start()
    loads[0].wait()
    loads[1].wait()
    top = top_ref[...]
    live = top >= 0
    grid_x = top >> 8
    grid_y = top & 255
    owner = jnp.where(live, (grid_x >> 6) * N_GY + (grid_y >> 4), -1)
    cells = (
        (grid_x & (BX - 1)) + 1,
        (grid_y & (BY - 1)) + 1,
        (front_ref[...] & (NZ - 1)) + 1,
    )
    cells = [cell.astype(F32) for cell in cells]

    before = iota((128, 256), 0) < iota((128, 256), 1)
    later = iota((128, 256), 1) >= 128
    counter = jnp.where(before | later, 1.0, 0.0).astype(BF16)
    seen = jnp.zeros((DEVICES, 128), F32)
    slot = iota((CAP, 128), 0)
    bounds = [seen]
    for k in range(CHUNKS):
        columns = slice(k * 128, (k + 1) * 128)
        mine = iota((DEVICES, 128), 0) == owner[k : k + 1, :]
        marks = jnp.where(mine, 1.0, 0.0).astype(BF16)
        marks_ref[:, columns] = marks
        counts = jnp.dot(marks, counter, preferred_element_type=F32)
        rank = jnp.sum(jnp.where(mine, counts[:, :128] + seen, 0.0), axis=0, keepdims=True)
        seen = seen + counts[:, 128:]
        rank_ref[pl.ds(k, 1), :] = rank
        here = slot == rank.astype(jnp.int32)
        for part in range(3):
            values_ref[part * CAP : (part + 1) * CAP, columns] = jnp.where(
                here, cells[part][k : k + 1, :], 0.0
            ).astype(BF16)
        if (k + 1) % GROUP_CHUNKS == 0:
            bounds.append(seen)

    below = jnp.where(iota((128, 128), 1) < iota((128, 128), 0), 1.0, 0.0).astype(BF16)
    diagonal = iota((128, 128), 0) == iota((128, 128), 1)
    for g in range(GROUPS):
        count = bounds[g + 1] - bounds[g]
        starts = jnp.dot(below, count.astype(BF16), preferred_element_type=F32)
        for row, numbers in ((g, starts), (GROUPS + g, bounds[g])):
            line = jnp.sum(jnp.where(diagonal, numbers, 0.0), axis=0, keepdims=True)
            start_ref[pl.ds(row, 1), :] = line.astype(jnp.int32)
        shift = starts - bounds[g]
        for k in range(g * GROUP_CHUNKS, (g + 1) * GROUP_CHUNKS):
            mine = iota((DEVICES, 128), 0) == owner[k : k + 1, :]
            place_ref[pl.ds(k, 1), :] = rank_ref[pl.ds(k, 1), :] + jnp.sum(
                jnp.where(mine, shift, 0.0), axis=0, keepdims=True
            )
    copy = pltpu.make_async_copy(start_ref, start_smem, sems.at[4])
    copy.start()
    place = place_ref[...].astype(jnp.int32)
    halves = columns_of(place // (GROUP // 2))
    rank_ref[...] = jnp.where(live, place & (GROUP // 2 - 1), -1).astype(F32)

    loads[2].wait()
    loads[3].wait()
    camera = embed_ref[pl.ds(cam_ref[0], 1), :]
    for k in range(CHUNKS):
        rows = slice(k * 128, (k + 1) * 128)
        features = (feats_ref[rows, :].astype(F32) + camera).astype(BF16)
        rhs_ref[rows, :] = split_columns(features, spread_column(halves, k))

    for g in range(GROUPS):
        points = rhs_ref[g * GROUP : (g + 1) * GROUP, :]
        labels = [rank_ref[pl.ds(g * GROUP_CHUNKS + k, 1), :].astype(jnp.int32) for k in range(GROUP_CHUNKS)]
        for base in range(0, GROUP // 2, 256):
            picked = jnp.dot(
                jnp.concatenate([onehot_rows(label, base, 256) for label in labels], axis=1),
                points,
                preferred_element_type=F32,
            )
            sorted_ref[g, base : base + 256, :] = picked[:, :C]
            sorted_ref[g, GROUP // 2 + base : GROUP // 2 + base + 256, :] = picked[:, C:]
        sorted_ref[g, GROUP : GROUP + CAP, :] = jnp.zeros((CAP, C), F32)

    meta = lax.dot_general(
        values_ref[...], marks_ref[...], (((1,), (1,)), ((), ())), preferred_element_type=F32
    )
    for part in range(3):
        numbers = meta[part * CAP : (part + 1) * CAP, :]
        meta_ref[pl.ds(part, DEVICES, stride=8), :] = jnp.concatenate([numbers, numbers], axis=0).T
    for part in range(3, 8):
        meta_ref[pl.ds(part, DEVICES, stride=8), :] = jnp.zeros((DEVICES, 128), F32)
    out_ref[:, CAP:ROWS, :] = meta_ref[...].reshape(DEVICES, 8, 128).astype(BF16)

    copy.wait()
    stores = []
    for part in range(4):

        @pl.loop(0, DEVICES // 4, unroll=8)
        def _(i):
            device = part * (DEVICES // 4) + i
            base = device * CAP
            for g in range(GROUPS):
                run = sorted_ref[g, pl.ds(start_smem[g, device], CAP), :]
                stage_ref[pl.ds(base + start_smem[GROUPS + g, device], CAP), :] = run
            out_ref[device, 0:CAP, :] = stage_ref[pl.ds(base, CAP), :].astype(BF16)

        here = pl.ds(part * (DEVICES // 4), DEVICES // 4)
        stores.append(pltpu.make_async_copy(out_ref.at[here], out_hbm.at[here], sems.at[5 + part]))
        stores[-1].start()
    for store in stores:
        store.wait()


def pack(camera, point_feats, top_bin, front_bin, camera_embed):
    whole = pl.BlockSpec(memory_space=pltpu.HBM)
    return pl.pallas_call(
        pack_kernel,
        out_shape=jax.ShapeDtypeStruct((DEVICES, ROWS, C), BF16),
        in_specs=[pl.BlockSpec(memory_space=pltpu.SMEM)] + [whole] * 4,
        out_specs=whole,
        scratch_shapes=[
            pltpu.VMEM((P_DEV, C), BF16),
            pltpu.VMEM((CHUNKS, 128), jnp.int32),
            pltpu.VMEM((CHUNKS, 128), jnp.int32),
            pltpu.VMEM((CAMS, C), F32),
            pltpu.VMEM((DEVICES, ROWS, C), BF16),
            pltpu.VMEM((DEVICES, P_DEV), BF16),
            pltpu.VMEM((CHUNKS, 128), F32),
            pltpu.VMEM((CHUNKS, 128), F32),
            pltpu.VMEM((P_DEV, 2 * C), BF16),
            pltpu.VMEM((3 * CAP, P_DEV), BF16),
            pltpu.VMEM((GROUPS, GROUP + CAP, C), F32),
            pltpu.VMEM((SLOTS + CAP, C), F32),
            pltpu.VMEM((DEVICES * 8, 128), F32),
            pltpu.VMEM((2 * GROUPS, DEVICES), jnp.int32),
            pltpu.SMEM((2 * GROUPS, DEVICES), jnp.int32),
            pltpu.SemaphoreType.DMA((9,)),
        ],
        compiler_params=pltpu.CompilerParams(vmem_limit_bytes=PACK_LIMIT),
        cost_estimate=pl.CostEstimate(flops=2 * 4096 * 4096 * 256, bytes_accessed=4 * 2**20, transcendentals=0),
        name="pack",
    )(camera, point_feats, top_bin.reshape(CHUNKS, 128), front_bin.reshape(CHUNKS, 128), camera_embed)


def split_points(got_ref, half_ref, rhs_ref):
    halves = columns_of(half_ref[...])
    for q in range(PAIRS):
        piece = got_ref[q * 2 : q * 2 + 2, 0:CAP, :].reshape(128, C)
        rhs_ref[q * 128 : (q + 1) * 128, :] = split_columns(piece, spread_column(halves, q))


def pool_front_kernel(place_ref, got_ref, mine_ref, other_ref, labels_ref, rhs_ref, meta_ref):
    meta_ref[...] = got_ref[:, CAP:ROWS, :].astype(F32).reshape(DEVICES * 8, 128)
    first = iota((PAIRS, 128), 1) < CAP

    def pairs(part):
        even = meta_ref[pl.ds(part, PAIRS, stride=16), :]
        odd = meta_ref[pl.ds(part + 8, PAIRS, stride=16), :]
        return jnp.where(first, even, odd).astype(jnp.int32) - 1

    x, y, z = pairs(0), pairs(1), pairs(2)
    live = x >= 0
    x = x ^ (place_ref[0] * (BX // 2))
    labels_ref[0] = jnp.where(live, x * 16 + (z & 15), -1)
    labels_ref[1] = jnp.where(live, x * 8 + (y & 7), -1)
    labels_ref[2] = jnp.where(live, (y ^ place_ref[1]) * 16 + (z & 15), -1)
    labels_ref[3] = (y >> 3) & 1
    labels_ref[4] = (z >> 4) & 1
    split_points(got_ref, labels_ref.at[4], rhs_ref)
    for block in range(4):
        sums = jnp.dot(onehot(labels_ref.at[0], block * 256, 256, PAIRS), rhs_ref[...], preferred_element_type=F32)
        out = (mine_ref, other_ref)[block // 2]
        xs = pl.ds(block % 2 * 16, 16)
        out[xs, 0:16, :] = sums[:, :C].reshape(16, 16, C)
        out[xs, 16:32, :] = sums[:, C:].reshape(16, 16, C)


def pool_side_kernel(rhs_ref, labels_ref, keep_ref, send_ref):
    sums = jnp.dot(onehot(labels_ref.at[2], 0, 256, PAIRS), rhs_ref[...], preferred_element_type=F32)
    for half, out in enumerate((keep_ref, send_ref)):
        rows = slice(half * 128, (half + 1) * 128)
        out[:, 0:16, :] = sums[rows, :C].reshape(BY // 2, 16, C)
        out[:, 16:32, :] = sums[rows, C:].reshape(BY // 2, 16, C)


def pool_top_kernel(got_ref, labels_ref, top_ref, rhs_ref):
    split_points(got_ref, labels_ref.at[3], rhs_ref)
    for block in range(2):
        sums = jnp.dot(onehot(labels_ref.at[1], block * 256, 256, PAIRS), rhs_ref[...], preferred_element_type=F32)
        halves = [sums[:, :C].reshape(32, 8, C), sums[:, C:].reshape(32, 8, C)]
        top_ref[pl.ds(block * 32, 32)] = jnp.concatenate(halves, axis=1).astype(BF16)


def call(kernel, ins, outs, scratch, flops, name):
    whole = pl.BlockSpec(memory_space=pltpu.VMEM)
    small = pl.BlockSpec(memory_space=pltpu.SMEM)
    return pl.pallas_call(
        kernel,
        out_shape=outs,
        in_specs=[small if i.dtype == jnp.int32 and i.size == 2 else whole for i in ins],
        out_specs=[whole] * len(outs),
        scratch_shapes=scratch,
        compiler_params=pltpu.CompilerParams(vmem_limit_bytes=VMEM_LIMIT),
        cost_estimate=pl.CostEstimate(flops=flops, bytes_accessed=flops // 1024, transcendentals=0),
        name=name,
    )(*ins)


def pool_front(place, got):
    shape = jax.ShapeDtypeStruct((BX // 2, NZ, C), F32)
    labels = jax.ShapeDtypeStruct((5, PAIRS, 128), jnp.int32)
    points = jax.ShapeDtypeStruct((SLOTS, 2 * C), BF16)
    scratch = [pltpu.VMEM((DEVICES * 8, 128), F32)]
    flops = 2 * 8192 * 1024 * 256 * 2
    return call(pool_front_kernel, [place, got], [shape, shape, labels, points], scratch, flops, "pool_front")


def pool_side(points, labels):
    shape = jax.ShapeDtypeStruct((BY // 2, NZ, C), F32)
    return call(pool_side_kernel, [points, labels], [shape, shape], [], 2 * 8192 * 512 * 256, "pool_side")


def pool_top(got, labels):
    return call(
        pool_top_kernel,
        [got, labels],
        [jax.ShapeDtypeStruct((BX, BY, C), BF16)],
        [pltpu.VMEM((SLOTS, 2 * C), BF16)],
        1024,
        "pool_top",
    )[0]


PIECE = 4
PIECES = BX // PIECE


def mlp_kernel(
    place_ref, top_ref, mine_ref, other_ref, near_ref, far_ref, w_in_ref, b_in_ref, w_out_ref, b_out_ref, out_hbm,
    side_ref, wide_ref, half_ref, out_ref, sems,
):
    for y in range(BY // 2):
        side_ref[y ^ place_ref[1]] = near_ref[y].astype(F32)
        side_ref[(y + BY // 2) ^ place_ref[1]] = far_ref[y].astype(F32)
    bias = b_in_ref[...]
    high = bias.astype(BF16).astype(F32)
    middle = (bias - high).astype(BF16).astype(F32)
    low = bias - high - middle
    row = iota((C, HID), 0)
    rest = jnp.where(row == 0, high, jnp.where(row == 1, middle, jnp.where(row == 2, low, 0.0)))
    wide_ref[0:C, :] = w_in_ref[...]
    wide_ref[C : 2 * C, :] = rest.astype(BF16)
    half_ref[...] = (w_out_ref[...].astype(F32) * 0.5).astype(BF16)

    def store(piece):
        return pltpu.make_async_copy(
            out_ref.at[pl.ds(piece * PIECE, PIECE)],
            out_hbm.at[pl.ds((piece ^ (place_ref[0] * (PIECES // 2))) * PIECE, PIECE)],
            sems.at[piece],
        )

    ones = jnp.where(iota((BY * NZ, C), 1) < 3, 1.0, 0.0).astype(BF16)
    for i in range(BX):
        top = top_ref[i].astype(F32)
        front = (mine_ref[i] if i < BX // 2 else other_ref[i - BX // 2]).astype(F32)
        cell = (top[:, None, :] + front[None, :, :] + side_ref[...]).astype(BF16).reshape(BY * NZ, C)
        inner = jnp.dot(jnp.concatenate([cell, ones], axis=1), wide_ref[...], preferred_element_type=F32)
        twice = (inner * (1.0 + lax.erf(inner * 0.7071067811865476))).astype(BF16)
        result = jnp.dot(twice, half_ref[...], preferred_element_type=F32)
        result = result + (b_out_ref[...] + cell.astype(F32))
        out_ref[i] = result.astype(BF16).reshape(BY, NZ, C)
        if i % PIECE == PIECE - 1:
            store(i // PIECE).start()
    for piece in range(PIECES):
        store(piece).wait()


def mlp(place, top, mine, other, near, far, w_in, b_in, w_out, b_out):
    whole = pl.BlockSpec(memory_space=pltpu.VMEM)
    return pl.pallas_call(
        mlp_kernel,
        in_specs=[pl.BlockSpec(memory_space=pltpu.SMEM)] + [whole] * 9,
        out_specs=pl.BlockSpec(memory_space=pl.ANY),
        scratch_shapes=[
            pltpu.VMEM((BY, NZ, C), F32),
            pltpu.VMEM((2 * C, HID), BF16),
            pltpu.VMEM((HID, C), BF16),
            pltpu.VMEM((BX, BY, NZ, C), BF16),
            pltpu.SemaphoreType.DMA((PIECES,)),
        ],
        out_shape=jax.ShapeDtypeStruct((BX, BY, NZ, C), BF16),
        compiler_params=pltpu.CompilerParams(vmem_limit_bytes=MLP_LIMIT),
        cost_estimate=pl.CostEstimate(
            flops=4 * BX * BY * NZ * C * HID, bytes_accessed=9 * 2**20, transcendentals=BX * BY * NZ * HID
        ),
        name="voxel_mlp",
    )(place, top, mine, other, near, far, w_in, b_in.reshape(1, HID), w_out, b_out.reshape(1, C))


SAME_CORE = [list(range(core, N_GY, 2)) for core in range(2)]


def swap(array, axis, size, bit):
    return lax.ppermute(array, axis, [(i, i ^ bit) for i in range(size)])


def spread_kernel(pieces_ref, out_ref):
    share = jnp.sum(pieces_ref[...], axis=0).astype(BF16)
    for i in range(8):
        out_ref[i] = share


def front_share(mine):
    pieces = mine.reshape(8, mine.shape[0] * mine.shape[1] // 8, C)
    pieces = lax.all_to_all(pieces, "gy", 0, 0, tiled=True, axis_index_groups=SAME_CORE)
    return call(spread_kernel, [pieces], [jax.ShapeDtypeStruct(pieces.shape, BF16)], [], 1024, "spread")[0]


def front_gather(copies):
    whole = lax.all_to_all(copies, "gy", 0, 0, tiled=True, axis_index_groups=SAME_CORE)
    return whole.reshape(BX // 2, NZ, C)


def sum_kernel(mine_ref, got_ref, out_ref):
    out_ref[...] = mine_ref[...] + got_ref[...]


def pair_sum(mine, got):
    return call(sum_kernel, [mine, got], [jax.ShapeDtypeStruct(mine.shape, F32)], [], 1024, "pair_sum")[0]


def side_near(keep, send):
    part = pair_sum(keep, swap(send, "gx", N_GX, 4))
    others = [swap(part, "gx", N_GX, bit) for bit in (2, 1, 3)]
    return (part + others[0] + others[1] + others[2]).astype(BF16)


def per_device(
    point_feats, top_bin, front_bin, side_bin, camera_of_device, camera_embed, w_in, b_in, w_out, b_out
):
    row = lax.axis_index("gx")
    place = jnp.stack(
        [lax.axis_index("gy") & 1, (row >> 2 & 1) * (BY // 2)]
    ).astype(jnp.int32)
    sent = pack(camera_of_device, point_feats, top_bin, front_bin, camera_embed)
    got = lax.all_to_all(sent, ("gx", "gy"), split_axis=0, concat_axis=0, tiled=True)
    mine, other, labels, points = pool_front(place, got)
    keep, send = pool_side(points, labels)
    mine = pair_sum(mine, swap(other, "gy", N_GY, 1))
    mine, keep, send = lax.optimization_barrier((mine, keep, send))
    top = pool_top(got, labels)
    front, near = lax.optimization_barrier((front_share(mine), side_near(keep, send)))
    mine = front_gather(front)
    mine, top, near, far = lax.optimization_barrier((mine, top, near, swap(near, "gx", N_GX, 4)))
    other = swap(mine, "gy", N_GY, 1)
    return mlp(place, top, mine, other, near, far, w_in, b_in, w_out, b_out)


def solution(mesh):
    points = P(("gx", "gy"))
    placed = (P(("gx", "gy"), None), points, points, points, points, P(), P(), P(), P(), P())
    return jax.shard_map(
        per_device, mesh=mesh, in_specs=placed, out_specs=P("gx", "gy", None, None), check_vma=False
    )
```

```python
import jax
import jax.numpy as jnp
from jax import lax
from jax.experimental import pallas as pl
from jax.experimental.pallas import tpu as pltpu
from jax.sharding import PartitionSpec as P

C = 128
HID = 256
CAMS = 6
NZ = 32
BX = 64
BY = 16
P_DEV = 4096
DEVICES = 128
N_GX = 8
N_GY = 16
CAP = 64
ROWS = CAP + 8
SLOTS = DEVICES * CAP
CHUNKS = P_DEV // 128
PAIRS = DEVICES // 2

F32 = jnp.float32
BF16 = jnp.bfloat16
VMEM_LIMIT = 24 * 2**20
PACK_LIMIT = 60 * 2**20
MLP_LIMIT = 40 * 2**20


def iota(shape, axis):
    return lax.broadcasted_iota(jnp.int32, shape, axis)


def columns_of(rows):
    padding = jnp.zeros((128 - rows.shape[0], 128), F32)
    return jnp.concatenate([rows.astype(F32), padding], axis=0).T


def spread_column(columns, k):
    return jnp.broadcast_to(columns[:, k : k + 1], (128, 128)).astype(BF16)


def split_columns(values, half):
    zero = jnp.zeros_like(values)
    left = half == jnp.zeros_like(half)
    return jnp.concatenate([jnp.where(left, values, zero), jnp.where(left, zero, values)], axis=1)


def onehot_rows(label, base, rows):
    return jnp.where(iota((rows, 128), 0) + base == label, 1.0, 0.0).astype(BF16)


def onehot(labels_ref, base, rows, chunks):
    return jnp.concatenate(
        [onehot_rows(labels_ref[pl.ds(k, 1), :], base, rows) for k in range(chunks)], axis=1
    )


GROUPS = 4
GROUP = P_DEV // GROUPS
GROUP_CHUNKS = GROUP // 128


def pack_kernel(
    cam_ref, feats_hbm, top_hbm, front_hbm, embed_hbm, out_hbm,
    feats_ref, top_ref, front_ref, embed_ref, out_ref,
    marks_ref, rank_ref, place_ref, rhs_ref, values_ref, sorted_ref, stage_ref, meta_ref, start_ref, start_smem, sems,
):
    loads = [
        pltpu.make_async_copy(source, target, sems.at[i])
        for i, (source, target) in enumerate(
            [(top_hbm, top_ref), (front_hbm, front_ref), (embed_hbm, embed_ref), (feats_hbm, feats_ref)]
        )
    ]
    for load in loads:
        load.start()
    loads[0].wait()
    loads[1].wait()
    top = top_ref[...]
    live = top >= 0
    grid_x = top >> 8
    grid_y = top & 255
    owner = jnp.where(live, (grid_x >> 6) * N_GY + (grid_y >> 4), -1)
    cells = (
        (grid_x & (BX - 1)) + 1,
        (grid_y & (BY - 1)) + 1,
        (front_ref[...] & (NZ - 1)) + 1,
    )
    cells = [cell.astype(F32) for cell in cells]

    before = iota((128, 256), 0) < iota((128, 256), 1)
    later = iota((128, 256), 1) >= 128
    counter = jnp.where(before | later, 1.0, 0.0).astype(BF16)
    seen = jnp.zeros((DEVICES, 128), F32)
    slot = iota((CAP, 128), 0)
    bounds = [seen]
    for k in range(CHUNKS):
        columns = slice(k * 128, (k + 1) * 128)
        mine = iota((DEVICES, 128), 0) == owner[k : k + 1, :]
        marks = jnp.where(mine, 1.0, 0.0).astype(BF16)
        marks_ref[:, columns] = marks
        counts = jnp.dot(marks, counter, preferred_element_type=F32)
        rank = jnp.sum(jnp.where(mine, counts[:, :128] + seen, 0.0), axis=0, keepdims=True)
        seen = seen + counts[:, 128:]
        rank_ref[pl.ds(k, 1), :] = rank
        here = slot == rank.astype(jnp.int32)
        for part in range(3):
            values_ref[part * CAP : (part + 1) * CAP, columns] = jnp.where(
                here, cells[part][k : k + 1, :], 0.0
            ).astype(BF16)
        if (k + 1) % GROUP_CHUNKS == 0:
            bounds.append(seen)

    below = jnp.where(iota((128, 128), 1) < iota((128, 128), 0), 1.0, 0.0).astype(BF16)
    diagonal = iota((128, 128), 0) == iota((128, 128), 1)
    for g in range(GROUPS):
        count = bounds[g + 1] - bounds[g]
        starts = jnp.dot(below, count.astype(BF16), preferred_element_type=F32)
        for row, numbers in ((g, starts), (GROUPS + g, bounds[g])):
            line = jnp.sum(jnp.where(diagonal, numbers, 0.0), axis=0, keepdims=True)
            start_ref[pl.ds(row, 1), :] = line.astype(jnp.int32)
        shift = starts - bounds[g]
        for k in range(g * GROUP_CHUNKS, (g + 1) * GROUP_CHUNKS):
            mine = iota((DEVICES, 128), 0) == owner[k : k + 1, :]
            place_ref[pl.ds(k, 1), :] = rank_ref[pl.ds(k, 1), :] + jnp.sum(
                jnp.where(mine, shift, 0.0), axis=0, keepdims=True
            )
    copy = pltpu.make_async_copy(start_ref, start_smem, sems.at[4])
    copy.start()
    place = place_ref[...].astype(jnp.int32)
    halves = columns_of(place // (GROUP // 2))
    rank_ref[...] = jnp.where(live, place & (GROUP // 2 - 1), -1).astype(F32)

    loads[2].wait()
    loads[3].wait()
    camera = embed_ref[pl.ds(cam_ref[0], 1), :]
    for k in range(CHUNKS):
        rows = slice(k * 128, (k + 1) * 128)
        features = (feats_ref[rows, :].astype(F32) + camera).astype(BF16)
        rhs_ref[rows, :] = split_columns(features, spread_column(halves, k))

    for g in range(GROUPS):
        points = rhs_ref[g * GROUP : (g + 1) * GROUP, :]
        labels = [rank_ref[pl.ds(g * GROUP_CHUNKS + k, 1), :].astype(jnp.int32) for k in range(GROUP_CHUNKS)]
        for base in range(0, GROUP // 2, 256):
            picked = jnp.dot(
                jnp.concatenate([onehot_rows(label, base, 256) for label in labels], axis=1),
                points,
                preferred_element_type=F32,
            )
            sorted_ref[g, base : base + 256, :] = picked[:, :C]
            sorted_ref[g, GROUP // 2 + base : GROUP // 2 + base + 256, :] = picked[:, C:]
        sorted_ref[g, GROUP : GROUP + CAP, :] = jnp.zeros((CAP, C), F32)

    meta = lax.dot_general(
        values_ref[...], marks_ref[...], (((1,), (1,)), ((), ())), preferred_element_type=F32
    )
    for part in range(3):
        numbers = meta[part * CAP : (part + 1) * CAP, :]
        meta_ref[pl.ds(part, DEVICES, stride=8), :] = jnp.concatenate([numbers, numbers], axis=0).T
    for part in range(3, 8):
        meta_ref[pl.ds(part, DEVICES, stride=8), :] = jnp.zeros((DEVICES, 128), F32)
    out_ref[:, CAP:ROWS, :] = meta_ref[...].reshape(DEVICES, 8, 128).astype(BF16)

    copy.wait()
    stores = []
    for part in range(4):

        @pl.loop(0, DEVICES // 4, unroll=8)
        def _(i):
            device = part * (DEVICES // 4) + i
            base = device * CAP
            for g in range(GROUPS):
                run = sorted_ref[g, pl.ds(start_smem[g, device], CAP), :]
                stage_ref[pl.ds(base + start_smem[GROUPS + g, device], CAP), :] = run
            out_ref[device, 0:CAP, :] = stage_ref[pl.ds(base, CAP), :].astype(BF16)

        here = pl.ds(part * (DEVICES // 4), DEVICES // 4)
        stores.append(pltpu.make_async_copy(out_ref.at[here], out_hbm.at[here], sems.at[5 + part]))
        stores[-1].start()
    for store in stores:
        store.wait()


def pack(camera, point_feats, top_bin, front_bin, camera_embed):
    whole = pl.BlockSpec(memory_space=pltpu.HBM)
    return pl.pallas_call(
        pack_kernel,
        out_shape=jax.ShapeDtypeStruct((DEVICES, ROWS, C), BF16),
        in_specs=[pl.BlockSpec(memory_space=pltpu.SMEM)] + [whole] * 4,
        out_specs=whole,
        scratch_shapes=[
            pltpu.VMEM((P_DEV, C), BF16),
            pltpu.VMEM((CHUNKS, 128), jnp.int32),
            pltpu.VMEM((CHUNKS, 128), jnp.int32),
            pltpu.VMEM((CAMS, C), F32),
            pltpu.VMEM((DEVICES, ROWS, C), BF16),
            pltpu.VMEM((DEVICES, P_DEV), BF16),
            pltpu.VMEM((CHUNKS, 128), F32),
            pltpu.VMEM((CHUNKS, 128), F32),
            pltpu.VMEM((P_DEV, 2 * C), BF16),
            pltpu.VMEM((3 * CAP, P_DEV), BF16),
            pltpu.VMEM((GROUPS, GROUP + CAP, C), F32),
            pltpu.VMEM((SLOTS + CAP, C), F32),
            pltpu.VMEM((DEVICES * 8, 128), F32),
            pltpu.VMEM((2 * GROUPS, DEVICES), jnp.int32),
            pltpu.SMEM((2 * GROUPS, DEVICES), jnp.int32),
            pltpu.SemaphoreType.DMA((9,)),
        ],
        compiler_params=pltpu.CompilerParams(vmem_limit_bytes=PACK_LIMIT),
        cost_estimate=pl.CostEstimate(flops=2 * 4096 * 4096 * 256, bytes_accessed=4 * 2**20, transcendentals=0),
        name="pack",
    )(camera, point_feats, top_bin.reshape(CHUNKS, 128), front_bin.reshape(CHUNKS, 128), camera_embed)


def split_points(got_ref, half_ref, rhs_ref):
    halves = columns_of(half_ref[...])
    for q in range(PAIRS):
        piece = got_ref[q * 2 : q * 2 + 2, 0:CAP, :].reshape(128, C)
        rhs_ref[q * 128 : (q + 1) * 128, :] = split_columns(piece, spread_column(halves, q))


def pool_front_kernel(place_ref, got_ref, mine_ref, other_ref, labels_ref, rhs_ref, meta_ref):
    meta_ref[...] = got_ref[:, CAP:ROWS, :].astype(F32).reshape(DEVICES * 8, 128)
    first = iota((PAIRS, 128), 1) < CAP

    def pairs(part):
        even = meta_ref[pl.ds(part, PAIRS, stride=16), :]
        odd = meta_ref[pl.ds(part + 8, PAIRS, stride=16), :]
        return jnp.where(first, even, odd).astype(jnp.int32) - 1

    x, y, z = pairs(0), pairs(1), pairs(2)
    live = x >= 0
    x = x ^ (place_ref[0] * (BX // 2))
    labels_ref[0] = jnp.where(live, x * 16 + (z & 15), -1)
    labels_ref[1] = jnp.where(live, x * 8 + (y & 7), -1)
    labels_ref[2] = jnp.where(live, (y ^ place_ref[1]) * 16 + (z & 15), -1)
    labels_ref[3] = (y >> 3) & 1
    labels_ref[4] = (z >> 4) & 1
    split_points(got_ref, labels_ref.at[4], rhs_ref)
    for block in range(4):
        sums = jnp.dot(onehot(labels_ref.at[0], block * 256, 256, PAIRS), rhs_ref[...], preferred_element_type=F32)
        out = (mine_ref, other_ref)[block // 2]
        xs = pl.ds(block % 2 * 16, 16)
        out[xs, 0:16, :] = sums[:, :C].reshape(16, 16, C)
        out[xs, 16:32, :] = sums[:, C:].reshape(16, 16, C)


def pool_side_kernel(rhs_ref, labels_ref, keep_ref, send_ref):
    sums = jnp.dot(onehot(labels_ref.at[2], 0, 256, PAIRS), rhs_ref[...], preferred_element_type=F32)
    for half, out in enumerate((keep_ref, send_ref)):
        rows = slice(half * 128, (half + 1) * 128)
        out[:, 0:16, :] = sums[rows, :C].reshape(BY // 2, 16, C)
        out[:, 16:32, :] = sums[rows, C:].reshape(BY // 2, 16, C)


def pool_top_kernel(got_ref, labels_ref, top_ref, rhs_ref):
    split_points(got_ref, labels_ref.at[3], rhs_ref)
    for block in range(2):
        sums = jnp.dot(onehot(labels_ref.at[1], block * 256, 256, PAIRS), rhs_ref[...], preferred_element_type=F32)
        halves = [sums[:, :C].reshape(32, 8, C), sums[:, C:].reshape(32, 8, C)]
        top_ref[pl.ds(block * 32, 32)] = jnp.concatenate(halves, axis=1).astype(BF16)


def call(kernel, ins, outs, scratch, flops, name):
    whole = pl.BlockSpec(memory_space=pltpu.VMEM)
    small = pl.BlockSpec(memory_space=pltpu.SMEM)
    return pl.pallas_call(
        kernel,
        out_shape=outs,
        in_specs=[small if i.dtype == jnp.int32 and i.size == 2 else whole for i in ins],
        out_specs=[whole] * len(outs),
        scratch_shapes=scratch,
        compiler_params=pltpu.CompilerParams(vmem_limit_bytes=VMEM_LIMIT),
        cost_estimate=pl.CostEstimate(flops=flops, bytes_accessed=flops // 1024, transcendentals=0),
        name=name,
    )(*ins)


def pool_front(place, got):
    shape = jax.ShapeDtypeStruct((BX // 2, NZ, C), F32)
    labels = jax.ShapeDtypeStruct((5, PAIRS, 128), jnp.int32)
    points = jax.ShapeDtypeStruct((SLOTS, 2 * C), BF16)
    scratch = [pltpu.VMEM((DEVICES * 8, 128), F32)]
    flops = 2 * 8192 * 1024 * 256 * 2
    return call(pool_front_kernel, [place, got], [shape, shape, labels, points], scratch, flops, "pool_front")


def pool_side(points, labels):
    shape = jax.ShapeDtypeStruct((BY // 2, NZ, C), F32)
    return call(pool_side_kernel, [points, labels], [shape, shape], [], 2 * 8192 * 512 * 256, "pool_side")


def pool_top(got, labels):
    return call(
        pool_top_kernel,
        [got, labels],
        [jax.ShapeDtypeStruct((BX, BY, C), BF16)],
        [pltpu.VMEM((SLOTS, 2 * C), BF16)],
        1024,
        "pool_top",
    )[0]


PIECE = 4
PIECES = BX // PIECE


def mlp_kernel(
    place_ref, top_ref, mine_ref, other_ref, near_ref, far_ref, w_in_ref, b_in_ref, w_out_ref, b_out_ref, out_hbm,
    side_ref, wide_ref, half_ref, out_ref, sems,
):
    for y in range(BY // 2):
        side_ref[y ^ place_ref[1]] = near_ref[y].astype(F32)
        side_ref[(y + BY // 2) ^ place_ref[1]] = far_ref[y].astype(F32)
    bias = b_in_ref[...]
    high = bias.astype(BF16).astype(F32)
    middle = (bias - high).astype(BF16).astype(F32)
    low = bias - high - middle
    row = iota((C, HID), 0)
    rest = jnp.where(row == 0, high, jnp.where(row == 1, middle, jnp.where(row == 2, low, 0.0)))
    wide_ref[0:C, :] = w_in_ref[...]
    wide_ref[C : 2 * C, :] = rest.astype(BF16)
    half_ref[...] = (w_out_ref[...].astype(F32) * 0.5).astype(BF16)

    def store(piece):
        return pltpu.make_async_copy(
            out_ref.at[pl.ds(piece * PIECE, PIECE)],
            out_hbm.at[pl.ds((piece ^ (place_ref[0] * (PIECES // 2))) * PIECE, PIECE)],
            sems.at[piece],
        )

    ones = jnp.where(iota((BY * NZ, C), 1) < 3, 1.0, 0.0).astype(BF16)
    for i in range(BX):
        top = top_ref[i].astype(F32)
        front = (mine_ref[i] if i < BX // 2 else other_ref[i - BX // 2]).astype(F32)
        cell = (top[:, None, :] + front[None, :, :] + side_ref[...]).astype(BF16).reshape(BY * NZ, C)
        inner = jnp.dot(jnp.concatenate([cell, ones], axis=1), wide_ref[...], preferred_element_type=F32)
        twice = (inner * (1.0 + lax.erf(inner * 0.7071067811865476))).astype(BF16)
        result = jnp.dot(twice, half_ref[...], preferred_element_type=F32)
        result = result + (b_out_ref[...] + cell.astype(F32))
        out_ref[i] = result.astype(BF16).reshape(BY, NZ, C)
        if i % PIECE == PIECE - 1:
            store(i // PIECE).start()
    for piece in range(PIECES):
        store(piece).wait()


def mlp(place, top, mine, other, near, far, w_in, b_in, w_out, b_out):
    whole = pl.BlockSpec(memory_space=pltpu.VMEM)
    return pl.pallas_call(
        mlp_kernel,
        in_specs=[pl.BlockSpec(memory_space=pltpu.SMEM)] + [whole] * 9,
        out_specs=pl.BlockSpec(memory_space=pl.ANY),
        scratch_shapes=[
            pltpu.VMEM((BY, NZ, C), F32),
            pltpu.VMEM((2 * C, HID), BF16),
            pltpu.VMEM((HID, C), BF16),
            pltpu.VMEM((BX, BY, NZ, C), BF16),
            pltpu.SemaphoreType.DMA((PIECES,)),
        ],
        out_shape=jax.ShapeDtypeStruct((BX, BY, NZ, C), BF16),
        compiler_params=pltpu.CompilerParams(vmem_limit_bytes=MLP_LIMIT),
        cost_estimate=pl.CostEstimate(
            flops=4 * BX * BY * NZ * C * HID, bytes_accessed=9 * 2**20, transcendentals=BX * BY * NZ * HID
        ),
        name="voxel_mlp",
    )(place, top, mine, other, near, far, w_in, b_in.reshape(1, HID), w_out, b_out.reshape(1, C))


SAME_CORE = [list(range(core, N_GY, 2)) for core in range(2)]


def swap(array, axis, size, bit):
    return lax.ppermute(array, axis, [(i, i ^ bit) for i in range(size)])


def spread_kernel(pieces_ref, out_ref):
    share = jnp.sum(pieces_ref[...], axis=0).astype(BF16)
    for i in range(8):
        out_ref[i] = share


def front_share(mine):
    pieces = mine.reshape(8, mine.shape[0] * mine.shape[1] // 8, C)
    pieces = lax.all_to_all(pieces, "gy", 0, 0, tiled=True, axis_index_groups=SAME_CORE)
    return call(spread_kernel, [pieces], [jax.ShapeDtypeStruct(pieces.shape, BF16)], [], 1024, "spread")[0]


def front_gather(copies):
    whole = lax.all_to_all(copies, "gy", 0, 0, tiled=True, axis_index_groups=SAME_CORE)
    return whole.reshape(BX // 2, NZ, C)


def sum_kernel(mine_ref, got_ref, out_ref):
    out_ref[...] = mine_ref[...] + got_ref[...]


def pair_sum(mine, got):
    return call(sum_kernel, [mine, got], [jax.ShapeDtypeStruct(mine.shape, F32)], [], 1024, "pair_sum")[0]


def side_near(keep, send):
    part = pair_sum(keep, swap(send, "gx", N_GX, 4))
    others = [swap(part, "gx", N_GX, bit) for bit in (2, 1, 3)]
    return (part + others[0] + others[1] + others[2]).astype(BF16)


def per_device(
    point_feats, top_bin, front_bin, side_bin, camera_of_device, camera_embed, w_in, b_in, w_out, b_out
):
    row = lax.axis_index("gx")
    place = jnp.stack(
        [lax.axis_index("gy") & 1, (row >> 2 & 1) * (BY // 2)]
    ).astype(jnp.int32)
    sent = pack(camera_of_device, point_feats, top_bin, front_bin, camera_embed)
    got = lax.all_to_all(sent, ("gx", "gy"), split_axis=0, concat_axis=0, tiled=True)
    mine, other, labels, points = pool_front(place, got)
    keep, send = pool_side(points, labels)
    mine, other, keep, send = lax.optimization_barrier((mine, swap(other, "gy", N_GY, 1), keep, send))
    mine = pair_sum(mine, other)
    top = pool_top(got, labels)
    front, near = lax.optimization_barrier((front_share(mine), side_near(keep, send)))
    mine = front_gather(front)
    mine, top, near, far = lax.optimization_barrier((mine, top, near, swap(near, "gx", N_GX, 4)))
    other = swap(mine, "gy", N_GY, 1)
    return mlp(place, top, mine, other, near, far, w_in, b_in, w_out, b_out)


def solution(mesh):
    points = P(("gx", "gy"))
    placed = (P(("gx", "gy"), None), points, points, points, points, P(), P(), P(), P(), P())
    return jax.shard_map(
        per_device, mesh=mesh, in_specs=placed, out_specs=P("gx", "gy", None, None), check_vma=False
    )
```
